512 devices in a mesh: ctx: 64 (over z, x), tp: 8 (over y, core).
Axes of the slice: x: 4, y: 4, z: 16, core: 2. Of those that a mesh axis runs over, the one named last changes fastest.
Arguments:
- features: bfloat16 [8192, 3, 4096], P('ctx', None, 'tp'), may hold values from -6 to 6
- short_filter: float32 [3, 3, 4096], P(None, None, 'tp'), may hold values from -3 to 3
- long_filter: float32 [8192, 4096], P('ctx', 'tp'), may hold values from -1.0558378 to 1.0558378
- filter_bias: float32 [4096], P('tp'), may hold values from -4 to 4
- out_weight: bfloat16 [4096, 4096], P('tp'), may hold values from -0.09375 to 0.09375
Outputs:
- mixed: bfloat16 [8192, 4096], P('ctx', 'tp')
The draws below stay inside these ranges and needn't reach their ends.
All inputs are finite; a program needn't handle non-finite values.
Results may differ from the reference program's by a relative error of at most 0.0049.
Values may be sent and summed in bfloat16 or wider, within the bound.
No kernel may reach another device: no remote copies, remote signals or barrier semaphores. Data moves between devices by JAX's collectives and lax.ppermute only.
A program may use at most 64 MiB of HBM per device.

```python
import math
import jax
import jax.numpy as jnp

MIXER_WIDTH = 4096
OUT_COLS = 4096
TAPS = 3
SEQUENCE_LENGTH = 8192


def draw_long_filter(key, part):
    random_keys = jax.random.split(key, 10)
    token_positions = jnp.arange(SEQUENCE_LENGTH, dtype=jnp.float32)[:, None]
    lowest = math.log(0.3 / SEQUENCE_LENGTH)
    log_rate = jax.random.uniform(random_keys[0], (1, MIXER_WIDTH), jnp.float32, lowest, math.log(1.0 / 30.0))
    noise = jnp.clip(jax.random.normal(random_keys[1], (SEQUENCE_LENGTH, MIXER_WIDTH), jnp.float32), -4.0, 4.0)
    rate = jnp.exp(log_rate)
    envelope = jnp.exp(-rate * token_positions)
    spike_location = jax.random.randint(random_keys[2], (3, MIXER_WIDTH), 0, SEQUENCE_LENGTH).astype(jnp.float32)
    spike_retained = jax.random.uniform(random_keys[3], (3, MIXER_WIDTH), jnp.float32, 0.5, 0.8)
    scale_factor = jnp.ones((SEQUENCE_LENGTH, MIXER_WIDTH), jnp.float32)
    for spike_train in range(3):
        scale_factor = scale_factor * jnp.where(token_positions >= spike_location[spike_train][None, :], spike_retained[spike_train][None, :], 1.0)
    scale = jnp.sqrt(2.0 * rate + 1.0 / SEQUENCE_LENGTH)
    tail_sign = jnp.where(jax.random.uniform(random_keys[6], (1, MIXER_WIDTH), jnp.float32) < 0.5, -1.0, 1.0)
    tail_amp = jax.random.uniform(random_keys[7], (1, MIXER_WIDTH), jnp.float32, 0.7, 1.4) * (0.9 / math.sqrt(SEQUENCE_LENGTH))
    tail_rate = jax.random.uniform(random_keys[8], (1, MIXER_WIDTH), jnp.float32, 0.0, 1.0 / SEQUENCE_LENGTH)
    tail_rough = jax.random.uniform(random_keys[9], (SEQUENCE_LENGTH, MIXER_WIDTH), jnp.float32, 0.5, 1.5)
    tail_part = tail_sign * tail_amp * tail_rough * jnp.exp(-tail_rate * token_positions)
    return ((noise * envelope * scale + tail_part) * scale_factor).astype(jnp.float32)


def block_scale(own_key, shape, cuts, least, largest):
    gain, own = 1.0, jax.random.fold_in(own_key, 6)
    for dim, shards_of in cuts:
        heights = jnp.exp(jax.random.uniform(jax.random.fold_in(own, dim), (shards_of,), jnp.float32, least / len(cuts), largest / len(cuts)))
        gain = gain * jnp.repeat(heights, shape[dim] // shards_of).reshape([-1 if axis == dim else 1 for axis in range(len(shape))])
    return gain


def normal_values(rng, shape, width, bound, shards=(), kind=jnp.bfloat16):
    level = block_scale(rng, shape, shards, -0.22, 0.18) if shards else 1.0
    values = jax.random.normal(rng, shape, jnp.float32) * width * level
    return jnp.minimum(jnp.maximum(values, -bound), bound).astype(kind)


def setup_inputs(seed: int = 0) -> dict:
    streams_of = jax.random.split(jax.random.key(seed), 6)
    return {
        "features": normal_values(streams_of[0], (SEQUENCE_LENGTH, 3, MIXER_WIDTH), 1.0, 6.0, ((0, 64), (2, 8))),
        "short_filter": normal_values(streams_of[1], (TAPS, 3, MIXER_WIDTH), 0.6, 3.0, ((2, 8),), jnp.float32),
        "long_filter": draw_long_filter(jax.random.fold_in(streams_of[5], 71), 0),
        "filter_bias": normal_values(streams_of[3], (MIXER_WIDTH,), 1.0, 4.0, ((0, 8),), jnp.float32),
        "out_weight": normal_values(streams_of[4], (MIXER_WIDTH, OUT_COLS), MIXER_WIDTH ** -0.5, 0.09375, ((0, 8),)),
    }


def reference(features, short_filter, long_filter, filter_bias, out_weight):
    current = features.astype(jnp.float32)
    padded = jnp.pad(current, ((2, 0), (0, 0), (0, 0)))
    seq_len = current.shape[0]
    featurized = short_filter[0] * current + short_filter[1] * padded[1:seq_len + 1] + short_filter[2] * padded[:seq_len]
    query_part = featurized[:, 0]
    key_part = featurized[:, 1]
    value_part = featurized[:, 2]
    gate_in = key_part * value_part
    full_len = 2 * seq_len
    gate_spec = jnp.fft.rfft(gate_in, n=full_len, axis=0)
    filter_spec = jnp.fft.rfft(long_filter, n=full_len, axis=0)
    long_conv = jnp.fft.irfft(gate_spec * filter_spec, n=full_len, axis=0)[:seq_len]
    long_conv = long_conv.astype(jnp.float32)
    conv_out = long_conv + filter_bias * gate_in
    gated = (query_part * conv_out).astype(jnp.bfloat16)
    return jnp.dot(gated, out_weight, preferred_element_type=jnp.float32).astype(jnp.bfloat16)
```

```python
import functools
import math

import jax
import jax.numpy as jnp
import numpy as np
from jax import lax
from jax.experimental import pallas as pl
from jax.experimental.pallas import tpu as pltpu
from jax.sharding import PartitionSpec as P

F32 = jnp.float32
BF16 = jnp.bfloat16
VMEM = pl.BlockSpec(memory_space=pltpu.VMEM)
PARAMS = pltpu.CompilerParams(vmem_limit_bytes=48 * 1024 * 1024)


def halves(table):
    high = table.astype(BF16)
    low = (table - high.astype(np.float32)).astype(BF16)
    return high, low


def tables(blocks, rows):
    length = blocks * rows
    freq = np.arange(blocks) + 0.25
    outer = 2.0 * math.pi * freq[:, None] * np.arange(blocks)[None, :] / blocks
    first = np.concatenate([np.cos(outer), -np.sin(outer)], axis=0).astype(np.float32)
    last = (np.concatenate([np.cos(outer.T), -np.sin(outer.T)], axis=1) / length).astype(np.float32)
    turn = 2.0 * math.pi * freq[:, None] * np.arange(rows)[None, :] / length
    twist = np.stack([np.cos(turn), np.sin(turn)]).astype(np.float32)
    inner = 2.0 * math.pi * (np.outer(np.arange(rows), np.arange(rows)) % rows) / rows
    cos, sin = np.cos(inner), np.sin(inner)
    forward = np.block([[cos, -sin], [sin, cos]]).astype(np.float32)
    backward = np.block([[cos, sin], [-sin, cos]]).astype(np.float32)
    first_hi, first_lo = halves(first)
    last_hi, last_lo = halves(last)
    forward_hi, forward_lo = halves(forward)
    backward_hi, backward_lo = halves(backward)
    return (
        np.concatenate([first_hi, first_lo], axis=1),
        twist,
        np.concatenate([forward_hi, forward_hi, forward_lo], axis=0),
        np.concatenate([backward_hi, backward_hi, backward_lo], axis=0),
        np.concatenate([last_hi, last_hi, last_lo], axis=1),
    )


def split(value):
    high = value.astype(BF16)
    return high, (value - high.astype(F32)).astype(BF16)


def short_kernel(features, rim, taps, filt, bias, send, query, skip):
    row = lax.broadcasted_iota(jnp.int32, features.shape[1:], 0)

    def stream(j):
        current = features[j].astype(F32)
        before = rim[j].astype(F32)
        one = jnp.where(row == 0, before[1:2], pltpu.roll(current, 1, 0))
        two = jnp.where(row == 0, before[0:1], jnp.where(row == 1, before[1:2], pltpu.roll(current, 2, 0)))
        return taps[0, j : j + 1] * current + taps[1, j : j + 1] * one + taps[2, j : j + 1] * two

    gate = stream(1) * stream(2)
    groups, both, rows = send.shape
    each = both // 2
    parts = [gate.T.reshape(groups, each, rows), filt[...].T.reshape(groups, each, rows)]
    send[...] = jnp.concatenate(parts, axis=1).astype(send.dtype)
    query[...] = stream(0).T
    skip[...] = (bias[...] * gate).T


def conv_kernel(columns, first, twist, forward, backward, last, out, gathered, spread):
    blocks, both, rows = columns.shape
    each = both // 2
    gathered[...] = columns[...].astype(F32).reshape(blocks * both, rows)
    wide = jnp.concatenate(
        [gathered[pl.ds(ch, blocks, stride=both), :] for ch in range(both)], axis=1
    ).astype(BF16)
    outer = jnp.dot(first[...], jnp.concatenate([wide, wide], axis=0), preferred_element_type=F32)
    cos, sin = twist[0], twist[1]
    twisted = []
    for ch in range(both):
        re = outer[:blocks, ch * rows : (ch + 1) * rows]
        im = outer[blocks:, ch * rows : (ch + 1) * rows]
        twisted.append(jnp.concatenate([re * cos + im * sin, im * cos - re * sin], axis=1))
    high, low = split(jnp.concatenate(twisted, axis=0))
    spectrum = jnp.dot(jnp.concatenate([high, low, high], axis=1), forward[...], preferred_element_type=F32)
    gate, filt = spectrum[: each * blocks], spectrum[each * blocks :]
    gate_re, gate_im = gate[:, :rows], gate[:, rows:]
    filt_re, filt_im = filt[:, :rows], filt[:, rows:]
    product = jnp.concatenate(
        [gate_re * filt_re - gate_im * filt_im, gate_re * filt_im + gate_im * filt_re], axis=1
    )
    high, low = split(product)
    inner = jnp.dot(jnp.concatenate([high, low, high], axis=1), backward[...], preferred_element_type=F32)
    turned = []
    for ch in range(each):
        re = inner[ch * blocks : (ch + 1) * blocks, :rows]
        im = inner[ch * blocks : (ch + 1) * blocks, rows:]
        turned.append(jnp.concatenate([re * cos - im * sin, re * sin + im * cos], axis=0))
    high, low = split(jnp.concatenate(turned, axis=1))
    result = jnp.dot(last[...], jnp.concatenate([high, low, high], axis=0), preferred_element_type=F32)
    for ch in range(each):
        spread[pl.ds(ch, blocks, stride=each), :] = result[:, ch * rows : (ch + 1) * rows]
    out[...] = spread[...].reshape(out.shape).astype(out.dtype)


def mix_kernel(conv, query, skip, weight, out, gated):
    @pl.when(pl.program_id(0) == 0)
    def _():
        conv_out = conv[...].astype(F32).reshape(query.shape) + skip[...]
        gated[...] = (query[...] * conv_out).T.astype(BF16)

    out[0] = jnp.dot(gated[...], weight[...], preferred_element_type=F32).astype(out.dtype)


def sum_kernel(parts, out):
    out[...] = jnp.sum(parts[...].astype(F32), axis=0).astype(out.dtype)


def body(features, short_filter, long_filter, filter_bias, out_weight):
    rows, streams, width = features.shape
    blocks = lax.axis_size("ctx")
    shares = lax.axis_size("tp")
    each = width // blocks
    cols = out_weight.shape[1] // shares
    planes = jnp.transpose(features, (1, 0, 2))
    route = [(i, i + 1) for i in range(blocks - 1)]
    rim = lax.ppermute(planes[:, rows - 2 :], "ctx", route)
    send, query, skip = pl.pallas_call(
        short_kernel,
        out_shape=(
            jax.ShapeDtypeStruct((blocks, 2 * each, rows), BF16),
            jax.ShapeDtypeStruct((width, rows), F32),
            jax.ShapeDtypeStruct((width, rows), F32),
        ),
        in_specs=[VMEM] * 5,
        out_specs=(VMEM, VMEM, VMEM),
        compiler_params=PARAMS,
        name="short",
    )(planes, rim, short_filter, long_filter, filter_bias.reshape(1, width))
    columns = lax.all_to_all(send, "ctx", split_axis=0, concat_axis=0, tiled=True)
    consts = [jnp.asarray(table) for table in tables(blocks, rows)]
    conv = pl.pallas_call(
        conv_kernel,
        out_shape=jax.ShapeDtypeStruct((blocks, each, rows), BF16),
        in_specs=[VMEM] * 6,
        out_specs=VMEM,
        scratch_shapes=[
            pltpu.VMEM((blocks * 2 * each, rows), F32),
            pltpu.VMEM((blocks * each, rows), F32),
        ],
        compiler_params=PARAMS,
        name="conv",
    )(columns, *consts)
    conv = lax.all_to_all(conv, "ctx", split_axis=0, concat_axis=0, tiled=True)
    whole = lambda shape: pl.BlockSpec(shape, lambda j: (0,) * len(shape))
    partial = pl.pallas_call(
        mix_kernel,
        grid=(shares,),
        out_shape=jax.ShapeDtypeStruct((shares, rows, cols), BF16),
        in_specs=[
            whole((blocks, each, rows)),
            whole((width, rows)),
            whole((width, rows)),
            pl.BlockSpec((width, cols), lambda j: (0, j)),
        ],
        out_specs=pl.BlockSpec((1, rows, cols), lambda j: (j, 0, 0)),
        scratch_shapes=[pltpu.VMEM((rows, width), BF16)],
        compiler_params=PARAMS,
        name="mix",
    )(conv, query, skip, out_weight)
    partial = lax.all_to_all(partial, "tp", split_axis=0, concat_axis=0, tiled=True)
    return pl.pallas_call(
        sum_kernel,
        out_shape=jax.ShapeDtypeStruct((rows, cols), BF16),
        in_specs=[VMEM],
        out_specs=VMEM,
        compiler_params=PARAMS,
        name="total",
    )(partial)


def solution(mesh):
    in_specs = (P("ctx", None, "tp"), P(None, None, "tp"), P("ctx", "tp"), P("tp"), P("tp", None))
    out_specs = P("ctx", "tp")
    return jax.shard_map(body, mesh=mesh, in_specs=in_specs, out_specs=out_specs, check_vma=False)
```

```python
import math

import jax
import jax.numpy as jnp
import numpy as np
from jax import lax
from jax.experimental import pallas as pl
from jax.experimental.pallas import tpu as pltpu
from jax.sharding import PartitionSpec as P

F32 = jnp.float32
BF16 = jnp.bfloat16
VMEM = pl.BlockSpec(memory_space=pltpu.VMEM)
PARAMS = pltpu.CompilerParams(vmem_limit_bytes=48 * 1024 * 1024)


def halves(table):
    high = table.astype(BF16)
    low = (table - high.astype(np.float32)).astype(BF16)
    return high, low


def tables(blocks, rows):
    length = blocks * rows
    freq = np.arange(blocks) + 0.25
    outer = 2.0 * math.pi * freq[:, None] * np.arange(blocks)[None, :] / blocks
    first = np.concatenate([np.cos(outer), -np.sin(outer)], axis=0).astype(np.float32)
    last = (np.concatenate([np.cos(outer.T), -np.sin(outer.T)], axis=1) / length).astype(np.float32)
    turn = 2.0 * math.pi * freq[:, None] * np.arange(rows)[None, :] / length
    twist = np.stack([np.cos(turn), np.sin(turn)]).astype(np.float32)
    inner = 2.0 * math.pi * (np.outer(np.arange(rows), np.arange(rows)) % rows) / rows
    cos, sin = np.cos(inner), np.sin(inner)
    forward = np.block([[cos, -sin], [sin, cos]]).astype(np.float32)
    backward = np.block([[cos, sin], [-sin, cos]]).astype(np.float32)
    first_hi, first_lo = halves(first)
    last_hi, last_lo = halves(last)
    forward_hi, forward_lo = halves(forward)
    backward_hi, backward_lo = halves(backward)
    return (
        np.concatenate([first_hi, first_lo], axis=1),
        twist,
        np.concatenate([forward_hi, forward_hi, forward_lo], axis=0),
        np.concatenate([backward_hi, backward_hi, backward_lo], axis=0),
        np.concatenate([last_hi, last_hi, last_lo], axis=1),
    )


def split(value):
    high = value.astype(BF16)
    return high, (value - high.astype(F32)).astype(BF16)


def stage_kernel(*refs):
    count = (len(refs) - 2) // 2
    filt, sources, columns, targets = refs[0], refs[1 : count], refs[count], refs[count + 1 : 2 * count]
    landed, sems = refs[2 * count :]
    load = pltpu.make_async_copy(filt, landed, sems.at[0])
    load.start()
    copies = []
    for i, (source, target) in enumerate(zip(sources, targets)):
        copies.append(pltpu.make_async_copy(source, target, sems.at[i + 1]))
        copies[-1].start()
    load.wait()
    columns[...] = landed[...].T.reshape(columns.shape).astype(columns.dtype)
    for copy in copies:
        copy.wait()


def short_kernel(features, rim, taps, filt, bias, send, query, skip):
    row = lax.broadcasted_iota(jnp.int32, features.shape[1:], 0)

    def stream(j):
        current = features[j].astype(F32)
        before = rim[j].astype(F32)
        one = jnp.where(row == 0, before[1:2], pltpu.roll(current, 1, 0))
        two = jnp.where(row == 0, before[0:1], jnp.where(row == 1, before[1:2], pltpu.roll(current, 2, 0)))
        return taps[0, j : j + 1] * current + taps[1, j : j + 1] * one + taps[2, j : j + 1] * two

    gate = stream(1) * stream(2)
    groups, both, rows = send.shape
    parts = [gate.T.reshape(groups, both // 2, rows), filt[...].astype(F32)]
    send[...] = jnp.concatenate(parts, axis=1).astype(send.dtype)
    query[...] = stream(0).T
    skip[...] = (bias[...] * gate).T


def conv_kernel(columns, first, twist, forward, backward, last, out, gathered, spread):
    blocks, both, rows = columns.shape
    each = both // 2
    gathered[...] = columns[...].astype(F32).reshape(blocks * both, rows)
    wide = jnp.concatenate(
        [gathered[pl.ds(ch, blocks, stride=both), :] for ch in range(both)], axis=1
    ).astype(BF16)
    outer = jnp.dot(first[...], jnp.concatenate([wide, wide], axis=0), preferred_element_type=F32)
    cos, sin = twist[0], twist[1]
    twisted = []
    for ch in range(both):
        re = outer[:blocks, ch * rows : (ch + 1) * rows]
        im = outer[blocks:, ch * rows : (ch + 1) * rows]
        twisted.append(jnp.concatenate([re * cos + im * sin, im * cos - re * sin], axis=1))
    high, low = split(jnp.concatenate(twisted, axis=0))
    spectrum = jnp.dot(jnp.concatenate([high, low, high], axis=1), forward[...], preferred_element_type=F32)
    gate, filt = spectrum[: each * blocks], spectrum[each * blocks :]
    gate_re, gate_im = gate[:, :rows], gate[:, rows:]
    filt_re, filt_im = filt[:, :rows], filt[:, rows:]
    product = jnp.concatenate(
        [gate_re * filt_re - gate_im * filt_im, gate_re * filt_im + gate_im * filt_re], axis=1
    )
    high, low = split(product)
    inner = jnp.dot(jnp.concatenate([high, low, high], axis=1), backward[...], preferred_element_type=F32)
    turned = []
    for ch in range(each):
        re = inner[ch * blocks : (ch + 1) * blocks, :rows]
        im = inner[ch * blocks : (ch + 1) * blocks, rows:]
        turned.append(jnp.concatenate([re * cos - im * sin, re * sin + im * cos], axis=0))
    high, low = split(jnp.concatenate(turned, axis=1))
    result = jnp.dot(last[...], jnp.concatenate([high, low, high], axis=0), preferred_element_type=F32)
    for ch in range(each):
        spread[pl.ds(ch, blocks, stride=each), :] = result[:, ch * rows : (ch + 1) * rows]
    out[...] = spread[...].reshape(out.shape).astype(out.dtype)


def gate_kernel(conv, query, skip, gated):
    conv_out = conv[...].astype(F32).reshape(query.shape) + skip[...]
    gated[...] = (query[...] * conv_out).T.astype(gated.dtype)


def core_columns(y, cols):
    core = lax.rem(lax.axis_index("tp"), 2)
    return pl.ds(pl.multiple_of((2 * y + core) * cols, cols), cols)


def own_kernel(gated, weight, partial, own, sems):
    chips, _, cols = partial.shape
    loads = [
        pltpu.make_async_copy(weight.at[:, core_columns(y, cols)], own.at[y], sems.at[y]) for y in range(chips)
    ]
    for load in loads:
        load.start()
    for y in range(chips):
        loads[y].wait()
        partial[y] = jnp.dot(gated[...], own[y], preferred_element_type=F32)


def both_kernel(gated, weight, partial, out):
    chips, _, cols = partial.shape
    for y in range(chips):
        added = jnp.dot(gated[...], weight[:, core_columns(y, cols)], preferred_element_type=F32)
        out[y] = (partial[y] + added).astype(out.dtype)


def sum_kernel(parts, out):
    out[...] = jnp.sum(parts[...].astype(F32), axis=0).astype(out.dtype)


def body(features, short_filter, long_filter, filter_bias, out_weight):
    rows, streams, width = features.shape
    blocks = lax.axis_size("ctx")
    shares = lax.axis_size("tp")
    chips = shares // 2
    each = width // blocks
    cols = out_weight.shape[1] // shares
    swap = [(i, i ^ 1) for i in range(shares)]
    other_weight = lax.ppermute(out_weight, "tp", swap)
    planes = jnp.transpose(features, (1, 0, 2))
    route = [(i, i + 1) for i in range(blocks - 1)]
    rim = lax.ppermute(planes[:, rows - 2 :], "ctx", route)
    consts = [jnp.asarray(table) for table in tables(blocks, rows)]
    staged = [planes, short_filter, filter_bias.reshape(1, width), *consts]
    filt, planes, taps, bias, *consts = pl.pallas_call(
        stage_kernel,
        out_shape=(
            jax.ShapeDtypeStruct((blocks, each, rows), BF16),
            *(jax.ShapeDtypeStruct(array.shape, array.dtype) for array in staged),
        ),
        in_specs=[pl.BlockSpec(memory_space=pltpu.HBM)] * (len(staged) + 1),
        out_specs=(VMEM,) * (len(staged) + 1),
        scratch_shapes=[pltpu.VMEM((rows, width), F32), pltpu.SemaphoreType.DMA((len(staged) + 1,))],
        compiler_params=PARAMS,
        name="stage",
    )(*(pltpu.with_memory_space_constraint(array, pltpu.HBM) for array in (long_filter, *staged)))
    send, query, skip = pl.pallas_call(
        short_kernel,
        out_shape=(
            jax.ShapeDtypeStruct((blocks, 2 * each, rows), BF16),
            jax.ShapeDtypeStruct((width, rows), F32),
            jax.ShapeDtypeStruct((width, rows), F32),
        ),
        in_specs=[VMEM] * 5,
        out_specs=(VMEM, VMEM, VMEM),
        compiler_params=PARAMS,
        name="short",
    )(planes, rim, taps, filt, bias)
    columns = lax.all_to_all(send, "ctx", split_axis=0, concat_axis=0, tiled=True)
    columns, other_weight = lax.optimization_barrier((columns, other_weight))
    conv = pl.pallas_call(
        conv_kernel,
        out_shape=jax.ShapeDtypeStruct((blocks, each, rows), BF16),
        in_specs=[VMEM] * 6,
        out_specs=VMEM,
        scratch_shapes=[
            pltpu.VMEM((blocks * 2 * each, rows), F32),
            pltpu.VMEM((blocks * each, rows), F32),
        ],
        compiler_params=PARAMS,
        name="conv",
    )(columns, *consts)
    conv = lax.all_to_all(conv, "ctx", split_axis=0, concat_axis=0, tiled=True)
    gated = pl.pallas_call(
        gate_kernel,
        out_shape=jax.ShapeDtypeStruct((rows, width), BF16),
        in_specs=[VMEM] * 3,
        out_specs=VMEM,
        compiler_params=PARAMS,
        name="gate",
    )(conv, query, skip)
    other_gated = lax.ppermute(gated, "tp", swap)
    partial = pl.pallas_call(
        own_kernel,
        out_shape=jax.ShapeDtypeStruct((chips, rows, cols), F32),
        in_specs=[VMEM, pl.BlockSpec(memory_space=pltpu.HBM)],
        out_specs=VMEM,
        scratch_shapes=[pltpu.VMEM((chips, width, cols), BF16), pltpu.SemaphoreType.DMA((chips,))],
        compiler_params=PARAMS,
        name="own",
    )(gated, pltpu.with_memory_space_constraint(out_weight, pltpu.HBM))
    partial = pl.pallas_call(
        both_kernel,
        out_shape=jax.ShapeDtypeStruct((chips, rows, cols), BF16),
        in_specs=[VMEM] * 3,
        out_specs=VMEM,
        compiler_params=PARAMS,
        name="both",
    )(other_gated, other_weight, partial)
    columns_of = [[2 * y + core for y in range(chips)] for core in range(2)]
    partial = lax.all_to_all(
        partial, "tp", split_axis=0, concat_axis=0, tiled=True, axis_index_groups=columns_of
    )
    return pl.pallas_call(
        sum_kernel,
        out_shape=jax.ShapeDtypeStruct((rows, cols), BF16),
        in_specs=[VMEM],
        out_specs=VMEM,
        compiler_params=PARAMS,
        name="total",
    )(partial)


def solution(mesh):
    in_specs = (P("ctx", None, "tp"), P(None, None, "tp"), P("ctx", "tp"), P("tp"), P("tp", None))
    out_specs = P("ctx", "tp")
    return jax.shard_map(body, mesh=mesh, in_specs=in_specs, out_specs=out_specs, check_vma=False)
```

```python
import functools
import math

import jax
import jax.numpy as jnp
import numpy as np
from jax import lax
from jax.experimental import pallas as pl
from jax.experimental.pallas import tpu as pltpu
from jax.sharding import PartitionSpec as P

F32 = jnp.float32
BF16 = jnp.bfloat16
VMEM = pl.BlockSpec(memory_space=pltpu.VMEM)
RIM = 16
PARAMS = pltpu.CompilerParams(vmem_limit_bytes=24 * 1024 * 1024)


def halves(table):
    high = table.astype(BF16)
    low = (table - high.astype(np.float32)).astype(BF16)
    return high, low


def tables(blocks, rows):
    length = blocks * rows
    freq = np.arange(blocks) + 0.25
    outer = 2.0 * math.pi * freq[:, None] * np.arange(blocks)[None, :] / blocks
    first = np.concatenate([np.cos(outer), -np.sin(outer)], axis=0).astype(np.float32)
    last = (np.concatenate([np.cos(outer.T), -np.sin(outer.T)], axis=1) / length).astype(np.float32)
    turn = 2.0 * math.pi * freq[:, None] * np.arange(rows)[None, :] / length
    twist = np.stack([np.cos(turn), np.sin(turn)]).astype(np.float32)
    inner = 2.0 * math.pi * (np.outer(np.arange(rows), np.arange(rows)) % rows) / rows
    cos, sin = np.cos(inner), np.sin(inner)
    forward = np.block([[cos, -sin], [sin, cos]]).astype(np.float32)
    backward = np.block([[cos, sin], [-sin, cos]]).astype(np.float32)
    first_hi, first_lo = halves(first)
    last_hi, last_lo = halves(last)
    forward_hi, forward_lo = halves(forward)
    backward_hi, backward_lo = halves(backward)
    return (
        np.concatenate([first_hi, first_lo], axis=1),
        twist,
        np.concatenate([forward_hi, forward_hi, forward_lo], axis=0),
        np.concatenate([backward_hi, backward_hi, backward_lo], axis=0),
        np.concatenate([last_hi, last_hi, last_lo], axis=1),
    )


def split(value):
    high = value.astype(BF16)
    return high, (value - high.astype(F32)).astype(BF16)


def load_all(sources, targets, sems):
    copies = [
        pltpu.make_async_copy(source, target, sems.at[i])
        for i, (source, target) in enumerate(zip(sources, targets))
    ]
    for copy in copies:
        copy.start()
    return copies


def short_kernel(count, *refs):
    inputs, (send, query, skip), tables = refs[:count], refs[count : count + 3], refs[count + 3 : 2 * count - 1]
    features, taps, filt, bias, wide, corner, sems = refs[2 * count - 1 :]
    copies = load_all(inputs, (features, taps, filt, bias, *tables), sems)
    for copy in copies[:4]:
        copy.wait()
    rows, width = filt.shape
    each = RIM // 2
    groups = width // each
    pitch = send.shape[0] // groups
    row = lax.broadcasted_iota(jnp.int32, (rows, width), 0)

    def stream(j):
        current = features[j].astype(F32)
        one = jnp.where(row == 0, 0.0, pltpu.roll(current, 1, 0))
        two = jnp.where(row < 2, 0.0, pltpu.roll(current, 2, 0))
        near, far = taps[1, j : j + 1], taps[2, j : j + 1]
        after = [near * current[rows - 1 :] + far * current[rows - 2 : rows - 1], far * current[rows - 1 :]]
        return taps[0, j : j + 1] * current + near * one + far * two, after

    asked, asked_after = stream(0)
    key, key_after = stream(1)
    value, value_after = stream(2)
    gate = key * value
    edge = [key[:2], value[:2], asked[:2], *key_after, *value_after, *asked_after, bias[...]]
    edge = jnp.concatenate([*edge, jnp.zeros((rows - 13, width), F32)], axis=0)
    corner[...] = edge.T
    lane = lax.broadcasted_iota(jnp.int32, (groups, rows), 1)
    packed = jnp.zeros((groups, rows), F32)
    for ch in range(each):
        mine = corner[pl.ds(ch, groups, stride=each), :]
        packed += jnp.where(lane // RIM == ch, pltpu.roll(mine, RIM * ch, 1) if ch else mine, 0.0)
    gate_t, filt_t = gate.T, filt[...].T
    for group in range(groups):
        wide[pitch * group : pitch * group + each] = gate_t[each * group : each * (group + 1)]
        wide[pitch * group + each : pitch * group + 2 * each] = filt_t[each * group : each * (group + 1)]
    wide[pl.ds(2 * each, groups, stride=pitch), :] = packed
    wide[pl.ds(2 * each + 1, groups, stride=pitch), :] = jnp.zeros((groups, rows), F32)
    send[...] = wide[...].astype(send.dtype)
    query[...] = asked.T
    skip[...] = (bias[...] * gate).T
    for copy in copies[4:]:
        copy.wait()


def conv_kernel(columns, first, twist, forward, backward, last, out, gathered, spread):
    each, blocks, rows = RIM // 2, out.shape[0], out.shape[2]
    both = 2 * each
    pitch = columns.shape[0] // blocks
    gathered[...] = columns[...].astype(F32)
    edge = gathered[pl.ds(both, blocks, stride=pitch), :]
    before = jnp.where(lax.broadcasted_iota(jnp.int32, edge.shape, 0) == 0, 0.0, pltpu.roll(edge, 1, 0))
    featurized = edge + pltpu.roll(before, rows - 6, 1)
    edge_gate = featurized * pltpu.roll(featurized, rows - 2, 1)
    edge_query = pltpu.roll(featurized, rows - 4, 1)
    edge_skip = pltpu.roll(edge, rows - 12, 1)
    lane = lax.broadcasted_iota(jnp.int32, edge.shape, 1)

    def channel(array, ch):
        return pltpu.roll(array, rows - RIM * ch, 1) if ch else array

    streams = [gathered[pl.ds(ch, blocks, stride=pitch), :] for ch in range(both)]
    for ch in range(each):
        streams[ch] = jnp.where(lane < 2, channel(edge_gate, ch), streams[ch])
    wide = jnp.concatenate(streams, axis=1).astype(BF16)
    outer = jnp.dot(first[...], jnp.concatenate([wide, wide], axis=0), preferred_element_type=F32)
    cos, sin = twist[0], twist[1]
    twisted = []
    for ch in range(both):
        re = outer[:blocks, ch * rows : (ch + 1) * rows]
        im = outer[blocks:, ch * rows : (ch + 1) * rows]
        twisted.append(jnp.concatenate([re * cos + im * sin, im * cos - re * sin], axis=1))
    high, low = split(jnp.concatenate(twisted, axis=0))
    spectrum = jnp.dot(jnp.concatenate([high, low, high], axis=1), forward[...], preferred_element_type=F32)
    gate, filt = spectrum[: each * blocks], spectrum[each * blocks :]
    gate_re, gate_im = gate[:, :rows], gate[:, rows:]
    filt_re, filt_im = filt[:, :rows], filt[:, rows:]
    product = jnp.concatenate(
        [gate_re * filt_re - gate_im * filt_im, gate_re * filt_im + gate_im * filt_re], axis=1
    )
    high, low = split(product)
    inner = jnp.dot(jnp.concatenate([high, low, high], axis=1), backward[...], preferred_element_type=F32)
    turned = []
    for ch in range(each):
        re = inner[ch * blocks : (ch + 1) * blocks, :rows]
        im = inner[ch * blocks : (ch + 1) * blocks, rows:]
        turned.append(jnp.concatenate([re * cos - im * sin, re * sin + im * cos], axis=0))
    high, low = split(jnp.concatenate(turned, axis=1))
    result = jnp.dot(last[...], jnp.concatenate([high, low, high], axis=0), preferred_element_type=F32)
    for ch in range(each):
        part = result[:, ch * rows : (ch + 1) * rows]
        scale = channel(edge_skip, ch)
        scale = jnp.where(lane == 1, pltpu.roll(scale, 1, 1), scale)
        finished = channel(edge_query, ch) * (part + scale * channel(edge_gate, ch))
        spread[pl.ds(ch, blocks, stride=each), :] = jnp.where(lane < 2, finished, part)
    out[...] = spread[...].reshape(out.shape).astype(out.dtype)


def gate_kernel(conv, query, skip, gated):
    arrived = conv[...].astype(F32).reshape(query.shape)
    row = lax.broadcasted_iota(jnp.int32, query.shape, 1)
    finished = jnp.where(row < 2, arrived, query[...] * (arrived + skip[...]))
    gated[...] = finished.T.astype(gated.dtype)


def core_columns(y, cols):
    core = lax.rem(lax.axis_index("tp"), 2)
    return pl.ds(pl.multiple_of((2 * y + core) * cols, cols), cols)


def own_kernel(gated, weight, other, partial, landed, own, sems):
    chips, _, cols = partial.shape
    sources = [array.at[:, core_columns(y, cols)] for array in (weight, other) for y in range(chips)]
    targets = [array.at[y] for array in (own, landed) for y in range(chips)]
    copies = load_all(sources, targets, sems)
    for y in range(chips):
        copies[y].wait()
        partial[y] = jnp.dot(gated[...], own[y], preferred_element_type=F32)
    for copy in copies[chips:]:
        copy.wait()


def both_kernel(gated, weight, partial, out):
    chips, _, cols = partial.shape
    for y in range(chips):
        added = jnp.dot(gated[...], weight[y], preferred_element_type=F32)
        out[y] = (partial[y] + added).astype(out.dtype)


def sum_kernel(parts, out):
    out[...] = jnp.sum(parts[...].astype(F32), axis=0).astype(out.dtype)


def body(features, short_filter, long_filter, filter_bias, out_weight):
    rows, streams, width = features.shape
    blocks = lax.axis_size("ctx")
    shares = lax.axis_size("tp")
    chips = shares // 2
    each = width // blocks
    cols = out_weight.shape[1] // shares
    swap = [(i, i ^ 1) for i in range(shares)]
    other_weight = lax.ppermute(out_weight, "tp", swap)
    consts = [jnp.asarray(table) for table in tables(blocks, rows)]
    planes = jnp.transpose(features, (1, 0, 2))
    staged = [planes, short_filter, long_filter, filter_bias.reshape(1, width), *consts]
    pitch = 2 * each + 2
    send, query, skip, *consts = pl.pallas_call(
        functools.partial(short_kernel, len(staged)),
        out_shape=(
            jax.ShapeDtypeStruct((blocks * pitch, rows), BF16),
            jax.ShapeDtypeStruct((width, rows), F32),
            jax.ShapeDtypeStruct((width, rows), F32),
            *(jax.ShapeDtypeStruct(array.shape, array.dtype) for array in consts),
        ),
        in_specs=[pl.BlockSpec(memory_space=pltpu.HBM)] * len(staged),
        out_specs=(VMEM,) * (3 + len(consts)),
        scratch_shapes=[
            *(pltpu.VMEM(array.shape, array.dtype) for array in staged[:4]),
            pltpu.VMEM((blocks * pitch, rows), F32),
            pltpu.VMEM((width, rows), F32),
            pltpu.SemaphoreType.DMA((len(staged),)),
        ],
        compiler_params=PARAMS,
        name="short",
    )(*(pltpu.with_memory_space_constraint(array, pltpu.HBM) for array in staged))
    send = send.reshape(blocks, pitch // 2, 2, rows)
    columns = lax.all_to_all(send, "ctx", split_axis=0, concat_axis=0, tiled=True)
    columns = columns.reshape(blocks * pitch, rows)
    columns, other_weight = lax.optimization_barrier((columns, other_weight))
    conv = pl.pallas_call(
        conv_kernel,
        out_shape=jax.ShapeDtypeStruct((blocks, each, rows), BF16),
        in_specs=[VMEM] * 6,
        out_specs=VMEM,
        scratch_shapes=[
            pltpu.VMEM((blocks * pitch, rows), F32),
            pltpu.VMEM((blocks * each, rows), F32),
        ],
        compiler_params=PARAMS,
        name="conv",
    )(columns, *consts)
    conv = lax.all_to_all(conv, "ctx", split_axis=0, concat_axis=0, tiled=True)
    gated = pl.pallas_call(
        gate_kernel,
        out_shape=jax.ShapeDtypeStruct((rows, width), BF16),
        in_specs=[VMEM] * 3,
        out_specs=VMEM,
        compiler_params=PARAMS,
        name="gate",
    )(conv, query, skip)
    other_gated = lax.ppermute(gated, "tp", swap)
    partial, landed = pl.pallas_call(
        own_kernel,
        out_shape=(
            jax.ShapeDtypeStruct((chips, rows, cols), F32),
            jax.ShapeDtypeStruct((chips, width, cols), BF16),
        ),
        in_specs=[VMEM] + [pl.BlockSpec(memory_space=pltpu.HBM)] * 2,
        out_specs=(VMEM, VMEM),
        scratch_shapes=[pltpu.VMEM((chips, width, cols), BF16), pltpu.SemaphoreType.DMA((2 * chips,))],
        compiler_params=PARAMS,
        name="own",
    )(gated, *(pltpu.with_memory_space_constraint(array, pltpu.HBM) for array in (out_weight, other_weight)))
    partial = pl.pallas_call(
        both_kernel,
        out_shape=jax.ShapeDtypeStruct((chips, rows, cols), BF16),
        in_specs=[VMEM] * 3,
        out_specs=VMEM,
        compiler_params=PARAMS,
        name="both",
    )(other_gated, landed, partial)
    columns_of = [[2 * y + core for y in range(chips)] for core in range(2)]
    partial = lax.all_to_all(
        partial, "tp", split_axis=0, concat_axis=0, tiled=True, axis_index_groups=columns_of
    )
    return pl.pallas_call(
        sum_kernel,
        out_shape=jax.ShapeDtypeStruct((rows, cols), BF16),
        in_specs=[VMEM],
        out_specs=VMEM,
        compiler_params=PARAMS,
        name="total",
    )(partial)


def solution(mesh):
    in_specs = (P("ctx", None, "tp"), P(None, None, "tp"), P("ctx", "tp"), P("tp"), P("tp", None))
    out_specs = P("ctx", "tp")
    return jax.shard_map(body, mesh=mesh, in_specs=in_specs, out_specs=out_specs, check_vma=False)
```

```python
import functools
import math

import jax
import jax.numpy as jnp
import numpy as np
from jax import lax
from jax.experimental import pallas as pl
from jax.experimental.pallas import tpu as pltpu
from jax.sharding import PartitionSpec as P

F32 = jnp.float32
BF16 = jnp.bfloat16
VMEM = pl.BlockSpec(memory_space=pltpu.VMEM)
RIM = 16
PARAMS = pltpu.CompilerParams(vmem_limit_bytes=24 * 1024 * 1024)


def halves(table):
    high = table.astype(BF16)
    low = (table - high.astype(np.float32)).astype(BF16)
    return high, low


def tables(blocks, rows):
    length = blocks * rows
    freq = np.arange(blocks) + 0.25
    outer = 2.0 * math.pi * freq[:, None] * np.arange(blocks)[None, :] / blocks
    first = np.concatenate([np.cos(outer), -np.sin(outer)], axis=0).astype(np.float32)
    last = (np.concatenate([np.cos(outer.T), -np.sin(outer.T)], axis=1) / length).astype(np.float32)
    turn = 2.0 * math.pi * freq[:, None] * np.arange(rows)[None, :] / length
    twist = np.stack([np.cos(turn), np.sin(turn)]).astype(np.float32)
    inner = 2.0 * math.pi * (np.outer(np.arange(rows), np.arange(rows)) % rows) / rows
    cos, sin = np.cos(inner), np.sin(inner)
    forward = np.block([[cos, -sin], [sin, cos]]).astype(np.float32)
    backward = np.block([[cos, sin], [-sin, cos]]).astype(np.float32)
    first_hi, first_lo = halves(first)
    last_hi, last_lo = halves(last)
    forward_hi, forward_lo = halves(forward)
    backward_hi, backward_lo = halves(backward)
    return (
        np.concatenate([first_hi, first_lo], axis=1),
        twist,
        np.concatenate([forward_hi, forward_hi, forward_lo], axis=0),
        np.concatenate([backward_hi, backward_hi, backward_lo], axis=0),
        np.concatenate([last_hi, last_hi, last_lo], axis=1),
    )


def split(value):
    high = value.astype(BF16)
    return high, (value - high.astype(F32)).astype(BF16)


def load_all(sources, targets, sems):
    copies = [
        pltpu.make_async_copy(source, target, sems.at[i])
        for i, (source, target) in enumerate(zip(sources, targets))
    ]
    for copy in copies:
        copy.start()
    return copies


def columns_of_core(weight, chips, partner):
    cols = weight.shape[1] // (2 * chips)
    core = lax.rem(lax.axis_index("tp") + partner, 2)
    return [weight.at[:, pl.ds(pl.multiple_of((2 * y + core) * cols, cols), cols)] for y in range(chips)]


def short_kernel(count, *refs):
    inputs, weight = refs[: count - 1], refs[count - 1]
    (send, query, skip, held), tables = refs[count : count + 4], refs[count + 4 : 2 * count - 1]
    features, taps, filt, bias, wide, corner, sems = refs[2 * count - 1 :]
    chips = held.shape[0]
    sources = [*inputs, *columns_of_core(weight, chips, 1)]
    copies = load_all(sources, (features, taps, filt, bias, *tables, *(held.at[y] for y in range(chips))), sems)
    for copy in copies[:4]:
        copy.wait()
    rows, width = filt.shape
    each = RIM // 2
    groups = width // each
    pitch = send.shape[0] // groups
    row = lax.broadcasted_iota(jnp.int32, (rows, width), 0)

    def stream(j):
        current = features[j].astype(F32)
        one = jnp.where(row == 0, 0.0, pltpu.roll(current, 1, 0))
        two = jnp.where(row < 2, 0.0, pltpu.roll(current, 2, 0))
        near, far = taps[1, j : j + 1], taps[2, j : j + 1]
        after = [near * current[rows - 1 :] + far * current[rows - 2 : rows - 1], far * current[rows - 1 :]]
        return taps[0, j : j + 1] * current + near * one + far * two, after

    asked, asked_after = stream(0)
    key, key_after = stream(1)
    value, value_after = stream(2)
    gate = key * value
    edge = [key[:2], value[:2], asked[:2], *key_after, *value_after, *asked_after, bias[...]]
    edge = jnp.concatenate([*edge, jnp.zeros((rows - 13, width), F32)], axis=0)
    corner[...] = edge.T
    lane = lax.broadcasted_iota(jnp.int32, (groups, rows), 1)
    packed = jnp.zeros((groups, rows), F32)
    for ch in range(each):
        mine = corner[pl.ds(ch, groups, stride=each), :]
        packed += jnp.where(lane // RIM == ch, pltpu.roll(mine, RIM * ch, 1) if ch else mine, 0.0)
    gate_t, filt_t = gate.T, filt[...].T
    for group in range(groups):
        wide[pitch * group : pitch * group + each] = gate_t[each * group : each * (group + 1)]
        wide[pitch * group + each : pitch * group + 2 * each] = filt_t[each * group : each * (group + 1)]
    wide[pl.ds(2 * each, groups, stride=pitch), :] = packed
    wide[pl.ds(2 * each + 1, groups, stride=pitch), :] = jnp.zeros((groups, rows), F32)
    send[...] = wide[...].astype(send.dtype)
    query[...] = asked.T
    skip[...] = (bias[...] * gate).T
    for copy in copies[4:]:
        copy.wait()


def conv_kernel(columns, first, twist, forward, backward, last, out, gathered, spread):
    each, blocks, rows = RIM // 2, out.shape[0], out.shape[2]
    both = 2 * each
    pitch = columns.shape[0] // blocks
    gathered[...] = columns[...].astype(F32)
    edge = gathered[pl.ds(both, blocks, stride=pitch), :]
    before = jnp.where(lax.broadcasted_iota(jnp.int32, edge.shape, 0) == 0, 0.0, pltpu.roll(edge, 1, 0))
    featurized = edge + pltpu.roll(before, rows - 6, 1)
    edge_gate = featurized * pltpu.roll(featurized, rows - 2, 1)
    edge_query = pltpu.roll(featurized, rows - 4, 1)
    edge_skip = pltpu.roll(edge, rows - 12, 1)
    lane = lax.broadcasted_iota(jnp.int32, edge.shape, 1)

    def channel(array, ch):
        return pltpu.roll(array, rows - RIM * ch, 1) if ch else array

    streams = [gathered[pl.ds(ch, blocks, stride=pitch), :] for ch in range(both)]
    for ch in range(each):
        streams[ch] = jnp.where(lane < 2, channel(edge_gate, ch), streams[ch])
    wide = jnp.concatenate(streams, axis=1).astype(BF16)
    outer = jnp.dot(first[...], jnp.concatenate([wide, wide], axis=0), preferred_element_type=F32)
    cos, sin = twist[0], twist[1]
    twisted = []
    for ch in range(both):
        re = outer[:blocks, ch * rows : (ch + 1) * rows]
        im = outer[blocks:, ch * rows : (ch + 1) * rows]
        twisted.append(jnp.concatenate([re * cos + im * sin, im * cos - re * sin], axis=1))
    high, low = split(jnp.concatenate(twisted, axis=0))
    spectrum = jnp.dot(jnp.concatenate([high, low, high], axis=1), forward[...], preferred_element_type=F32)
    gate, filt = spectrum[: each * blocks], spectrum[each * blocks :]
    gate_re, gate_im = gate[:, :rows], gate[:, rows:]
    filt_re, filt_im = filt[:, :rows], filt[:, rows:]
    product = jnp.concatenate(
        [gate_re * filt_re - gate_im * filt_im, gate_re * filt_im + gate_im * filt_re], axis=1
    )
    high, low = split(product)
    inner = jnp.dot(jnp.concatenate([high, low, high], axis=1), backward[...], preferred_element_type=F32)
    turned = []
    for ch in range(each):
        re = inner[ch * blocks : (ch + 1) * blocks, :rows]
        im = inner[ch * blocks : (ch + 1) * blocks, rows:]
        turned.append(jnp.concatenate([re * cos - im * sin, re * sin + im * cos], axis=0))
    high, low = split(jnp.concatenate(turned, axis=1))
    result = jnp.dot(last[...], jnp.concatenate([high, low, high], axis=0), preferred_element_type=F32)
    for ch in range(each):
        part = result[:, ch * rows : (ch + 1) * rows]
        scale = channel(edge_skip, ch)
        scale = jnp.where(lane == 1, pltpu.roll(scale, 1, 1), scale)
        finished = channel(edge_query, ch) * (part + scale * channel(edge_gate, ch))
        spread[pl.ds(ch, blocks, stride=each), :] = jnp.where(lane < 2, finished, part)
    out[...] = spread[...].reshape(out.shape).astype(out.dtype)


def give_kernel(conv, query, skip, weight, gated, given):
    arrived = conv[...].astype(F32).reshape(query.shape)
    row = lax.broadcasted_iota(jnp.int32, query.shape, 1)
    finished = jnp.where(row < 2, arrived, query[...] * (arrived + skip[...]))
    gated[...] = finished.T.astype(gated.dtype)
    for y in range(given.shape[0]):
        given[y] = jnp.dot(gated[...], weight[y], preferred_element_type=F32).astype(given.dtype)


def keep_kernel(gated, weight, kept, held, sems):
    chips = kept.shape[0]
    copies = load_all(columns_of_core(weight, chips, 0), [held.at[y] for y in range(chips)], sems)
    for y in range(chips):
        copies[y].wait()
        kept[y] = jnp.dot(gated[...], held[y], preferred_element_type=F32)


def pair_kernel(kept, arrived, out):
    out[...] = (kept[...] + arrived[...].astype(F32)).astype(out.dtype)


def sum_kernel(parts, out):
    out[...] = jnp.sum(parts[...].astype(F32), axis=0).astype(out.dtype)


def body(features, short_filter, long_filter, filter_bias, out_weight):
    rows, streams, width = features.shape
    blocks = lax.axis_size("ctx")
    shares = lax.axis_size("tp")
    chips = shares // 2
    each = width // blocks
    cols = out_weight.shape[1] // shares
    consts = [jnp.asarray(table) for table in tables(blocks, rows)]
    planes = jnp.transpose(features, (1, 0, 2))
    staged = [planes, short_filter, long_filter, filter_bias.reshape(1, width), *consts, out_weight]
    pitch = 2 * each + 2
    send, query, skip, held, *consts = pl.pallas_call(
        functools.partial(short_kernel, len(staged)),
        out_shape=(
            jax.ShapeDtypeStruct((blocks * pitch, rows), BF16),
            jax.ShapeDtypeStruct((width, rows), F32),
            jax.ShapeDtypeStruct((width, rows), F32),
            jax.ShapeDtypeStruct((chips, width, cols), BF16),
            *(jax.ShapeDtypeStruct(array.shape, array.dtype) for array in consts),
        ),
        in_specs=[pl.BlockSpec(memory_space=pltpu.HBM)] * len(staged),
        out_specs=(VMEM,) * (4 + len(consts)),
        scratch_shapes=[
            *(pltpu.VMEM(array.shape, array.dtype) for array in staged[:4]),
            pltpu.VMEM((blocks * pitch, rows), F32),
            pltpu.VMEM((width, rows), F32),
            pltpu.SemaphoreType.DMA((len(staged) - 1 + chips,)),
        ],
        compiler_params=PARAMS,
        name="short",
    )(*(pltpu.with_memory_space_constraint(array, pltpu.HBM) for array in staged))
    send = send.reshape(blocks, pitch // 2, 2, rows)
    columns = lax.all_to_all(send, "ctx", split_axis=0, concat_axis=0, tiled=True)
    columns = columns.reshape(blocks * pitch, rows)
    conv = pl.pallas_call(
        conv_kernel,
        out_shape=jax.ShapeDtypeStruct((blocks, each, rows), BF16),
        in_specs=[VMEM] * 6,
        out_specs=VMEM,
        scratch_shapes=[
            pltpu.VMEM((blocks * pitch, rows), F32),
            pltpu.VMEM((blocks * each, rows), F32),
        ],
        compiler_params=PARAMS,
        name="conv",
    )(columns, *consts)
    conv = lax.all_to_all(conv, "ctx", split_axis=0, concat_axis=0, tiled=True)
    gated, given = pl.pallas_call(
        give_kernel,
        out_shape=(
            jax.ShapeDtypeStruct((rows, width), BF16),
            jax.ShapeDtypeStruct((chips, rows, cols), BF16),
        ),
        in_specs=[VMEM] * 4,
        out_specs=(VMEM, VMEM),
        compiler_params=PARAMS,
        name="give",
    )(conv, query, skip, held)
    arrived = lax.ppermute(given, "tp", [(i, i ^ 1) for i in range(shares)])
    kept = pl.pallas_call(
        keep_kernel,
        out_shape=jax.ShapeDtypeStruct((chips, rows, cols), F32),
        in_specs=[VMEM, pl.BlockSpec(memory_space=pltpu.HBM)],
        out_specs=VMEM,
        scratch_shapes=[pltpu.VMEM((chips, width, cols), BF16), pltpu.SemaphoreType.DMA((chips,))],
        compiler_params=PARAMS,
        name="keep",
    )(gated, pltpu.with_memory_space_constraint(out_weight, pltpu.HBM))
    partial = pl.pallas_call(
        pair_kernel,
        out_shape=jax.ShapeDtypeStruct((chips, rows, cols), BF16),
        in_specs=[VMEM] * 2,
        out_specs=VMEM,
        compiler_params=PARAMS,
        name="pair",
    )(kept, arrived)
    columns_of = [[2 * y + core for y in range(chips)] for core in range(2)]
    partial = lax.all_to_all(
        partial, "tp", split_axis=0, concat_axis=0, tiled=True, axis_index_groups=columns_of
    )
    return pl.pallas_call(
        sum_kernel,
        out_shape=jax.ShapeDtypeStruct((rows, cols), BF16),
        in_specs=[VMEM],
        out_specs=VMEM,
        compiler_params=PARAMS,
        name="total",
    )(partial)


def solution(mesh):
    in_specs = (P("ctx", None, "tp"), P(None, None, "tp"), P("ctx", "tp"), P("tp"), P("tp", None))
    out_specs = P("ctx", "tp")
    return jax.shard_map(body, mesh=mesh, in_specs=in_specs, out_specs=out_specs, check_vma=False)
```

```python
import functools
import math

import jax
import jax.numpy as jnp
import numpy as np
from jax import lax
from jax.experimental import pallas as pl
from jax.experimental.pallas import tpu as pltpu
from jax.sharding import PartitionSpec as P

F32 = jnp.float32
BF16 = jnp.bfloat16
VMEM = pl.BlockSpec(memory_space=pltpu.VMEM)
RIM = 16
SIDE = 4
PARAMS = pltpu.CompilerParams(vmem_limit_bytes=24 * 1024 * 1024)


def halves(table):
    high = table.astype(BF16)
    low = (table - high.astype(np.float32)).astype(BF16)
    return high, low


def block_order(blocks):
    return np.arange(blocks).reshape(-1, SIDE).T.reshape(-1)


def tables(blocks, rows):
    length = blocks * rows
    freq = np.arange(blocks) + 0.25
    outer = 2.0 * math.pi * freq[:, None] * block_order(blocks)[None, :] / blocks
    first = np.concatenate([np.cos(outer), -np.sin(outer)], axis=0).astype(np.float32)
    last = (np.concatenate([np.cos(outer.T), -np.sin(outer.T)], axis=1) / length).astype(np.float32)
    turn = 2.0 * math.pi * freq[:, None] * np.arange(rows)[None, :] / length
    twist = np.stack([np.cos(turn), np.sin(turn)]).astype(np.float32)
    inner = 2.0 * math.pi * (np.outer(np.arange(rows), np.arange(rows)) % rows) / rows
    cos, sin = np.cos(inner), np.sin(inner)
    forward = np.block([[cos, -sin], [sin, cos]]).astype(np.float32)
    first_hi, first_lo = halves(first)
    last_hi, last_lo = halves(last)
    forward_hi, forward_lo = halves(forward)
    return (
        np.concatenate([first_hi, first_lo], axis=1),
        twist,
        np.stack([forward_hi, forward_lo]),
        np.concatenate([last_hi, last_hi, last_lo], axis=1),
    )


def transform(value, matrix):
    high, low = split(value)
    total = jnp.dot(high, matrix[0], preferred_element_type=F32)
    total += jnp.dot(low, matrix[0], preferred_element_type=F32)
    return total + jnp.dot(high, matrix[1], preferred_element_type=F32)


def split(value):
    high = value.astype(BF16)
    return high, (value - high.astype(F32)).astype(BF16)


def load_all(sources, targets, sems):
    copies = [
        pltpu.make_async_copy(source, target, sems.at[i])
        for i, (source, target) in enumerate(zip(sources, targets))
    ]
    for copy in copies:
        copy.start()
    return copies


def columns_of_core(weight, chips, partner):
    cols = weight.shape[1] // (2 * chips)
    core = lax.rem(lax.axis_index("tp") + partner, 2)
    return [weight.at[:, pl.ds(pl.multiple_of((2 * y + core) * cols, cols), cols)] for y in range(chips)]


def short_kernel(count, *refs):
    inputs, weight = refs[: count - 1], refs[count - 1]
    (send, query, skip, held), tables = refs[count : count + 4], refs[count + 4 : 2 * count - 1]
    features, taps, filt, bias, wide, corner, sems = refs[2 * count - 1 :]
    chips = held.shape[0]
    sources = [*inputs, *columns_of_core(weight, chips, 1)]
    copies = load_all(sources, (features, taps, filt, bias, *tables, *(held.at[y] for y in range(chips))), sems)
    for copy in copies[:4]:
        copy.wait()
    rows, width = filt.shape
    each = RIM // 2
    groups = width // each
    pitch = send.shape[0] // groups
    row = lax.broadcasted_iota(jnp.int32, (rows, width), 0)

    def stream(j):
        current = features[j].astype(F32)
        one = jnp.where(row == 0, 0.0, pltpu.roll(current, 1, 0))
        two = jnp.where(row < 2, 0.0, pltpu.roll(current, 2, 0))
        near, far = taps[1, j : j + 1], taps[2, j : j + 1]
        after = [near * current[rows - 1 :] + far * current[rows - 2 : rows - 1], far * current[rows - 1 :]]
        return taps[0, j : j + 1] * current + near * one + far * two, after

    asked, asked_after = stream(0)
    key, key_after = stream(1)
    value, value_after = stream(2)
    gate = key * value
    edge = [key[:2], value[:2], asked[:2], *key_after, *value_after, *asked_after, bias[...], bias[...]]
    edge = jnp.concatenate([*edge, jnp.zeros((RIM - 14, width), F32)], axis=0)
    corner[:, :RIM] = edge.T
    lane = lax.broadcasted_iota(jnp.int32, (groups, rows), 1)
    packed = jnp.zeros((groups, rows), F32)
    for ch in range(each):
        mine = corner[pl.ds(ch, groups, stride=each), :]
        packed += jnp.where(lane // RIM == ch, pltpu.roll(mine, RIM * ch, 1) if ch else mine, 0.0)
    gate_t, filt_t = gate.T, filt[...].T
    for group in range(groups):
        wide[pitch * group : pitch * group + each] = gate_t[each * group : each * (group + 1)]
        wide[pitch * group + each : pitch * group + 2 * each] = filt_t[each * group : each * (group + 1)]
    wide[pl.ds(2 * each, groups, stride=pitch), :] = packed
    wide[pl.ds(2 * each + 1, groups, stride=pitch), :] = jnp.zeros((groups, rows), F32)
    send[...] = wide[...].astype(send.dtype)
    query[...] = asked
    skip[...] = bias[...] * gate
    for copy in copies[4:]:
        copy.wait()


def conv_kernel(columns, first, twist, forward, last, out, gathered, spread):
    each, blocks, rows = RIM // 2, out.shape[0], out.shape[2]
    both = 2 * each
    pitch = columns.shape[0] // blocks
    gathered[...] = columns[...].astype(F32)
    edge = gathered[pl.ds(both, blocks, stride=pitch), :]
    deep = blocks // SIDE
    wrapped = pltpu.roll(edge[blocks - deep :], 1, 0)
    wrapped = jnp.where(lax.broadcasted_iota(jnp.int32, wrapped.shape, 0) == 0, 0.0, wrapped)
    before = jnp.concatenate([wrapped, edge[: blocks - deep]], axis=0)
    featurized = edge + pltpu.roll(before, rows - 6, 1)
    edge_gate = featurized * pltpu.roll(featurized, rows - 2, 1)
    edge_query = pltpu.roll(featurized, rows - 4, 1)
    edge_skip = edge_query * edge_gate * pltpu.roll(edge, rows - 12, 1)
    lane = lax.broadcasted_iota(jnp.int32, edge.shape, 1)

    def channel(array, ch):
        return pltpu.roll(array, rows - RIM * ch, 1) if ch else array

    streams = [gathered[pl.ds(ch, blocks, stride=pitch), :] for ch in range(both)]
    for ch in range(each):
        streams[ch] = jnp.where(lane < 2, channel(edge_gate, ch), streams[ch])
    wide = jnp.concatenate(streams, axis=1).astype(BF16)
    outer = jnp.dot(first[...], jnp.concatenate([wide, wide], axis=0), preferred_element_type=F32)
    cos, sin = twist[0], twist[1]
    twisted = []
    for ch in range(both):
        re = outer[:blocks, ch * rows : (ch + 1) * rows]
        im = outer[blocks:, ch * rows : (ch + 1) * rows]
        twisted.append(jnp.concatenate([re * cos + im * sin, im * cos - re * sin], axis=1))
    spectrum = transform(jnp.concatenate(twisted, axis=0), forward)
    gate, filt = spectrum[: each * blocks], spectrum[each * blocks :]
    gate_re, gate_im = gate[:, :rows], gate[:, rows:]
    filt_re, filt_im = filt[:, :rows], filt[:, rows:]
    product = [gate_re * filt_re - gate_im * filt_im, -gate_re * filt_im - gate_im * filt_re]
    inner = transform(jnp.concatenate(product, axis=1), forward)
    turned = []
    for ch in range(each):
        re = inner[ch * blocks : (ch + 1) * blocks, :rows]
        im = inner[ch * blocks : (ch + 1) * blocks, rows:]
        turned.append(jnp.concatenate([re * cos + im * sin, re * sin - im * cos], axis=0))
    high, low = split(jnp.concatenate(turned, axis=1))
    result = jnp.dot(last[...], jnp.concatenate([high, low, high], axis=0), preferred_element_type=F32)
    for ch in range(each):
        part = result[:, ch * rows : (ch + 1) * rows]
        finished = channel(edge_query, ch) * part + channel(edge_skip, ch)
        spread[pl.ds(ch, blocks, stride=each), :] = jnp.where(lane < 2, finished, part)
    out[...] = spread[...].reshape(out.shape).astype(out.dtype)


def give_kernel(conv, query, skip, weight, gated, given):
    arrived = conv[...].astype(F32).reshape(query.shape[::-1]).T
    row = lax.broadcasted_iota(jnp.int32, query.shape, 0)
    finished = jnp.where(row < 2, arrived, query[...] * (arrived + skip[...]))
    gated[...] = finished.astype(gated.dtype)
    for y in range(given.shape[0]):
        given[y] = jnp.dot(gated[...], weight[y], preferred_element_type=F32).astype(given.dtype)


def keep_kernel(gated, weight, kept, held, sems):
    chips = kept.shape[0]
    copies = load_all(columns_of_core(weight, chips, 0), [held.at[y] for y in range(chips)], sems)
    for y in range(chips):
        copies[y].wait()
        kept[y] = jnp.dot(gated[...], held[y], preferred_element_type=F32)


def pair_kernel(kept, arrived, out):
    out[...] = (kept[...] + arrived[...].astype(F32)).astype(out.dtype)


def sum_kernel(parts, out):
    out[...] = jnp.sum(parts[...].astype(F32), axis=0).astype(out.dtype)


def body(features, short_filter, long_filter, filter_bias, out_weight):
    rows, streams, width = features.shape
    blocks = lax.axis_size("ctx")
    shares = lax.axis_size("tp")
    chips = shares // 2
    each = width // blocks
    order = [[int(block) for block in block_order(blocks)]]
    cols = out_weight.shape[1] // shares
    consts = [jnp.asarray(table) for table in tables(blocks, rows)]
    planes = jnp.transpose(features, (1, 0, 2))
    staged = [planes, short_filter, long_filter, filter_bias.reshape(1, width), *consts, out_weight]
    pitch = 2 * each + 2
    send, query, skip, held, *consts = pl.pallas_call(
        functools.partial(short_kernel, len(staged)),
        out_shape=(
            jax.ShapeDtypeStruct((blocks * pitch, rows), BF16),
            jax.ShapeDtypeStruct((rows, width), F32),
            jax.ShapeDtypeStruct((rows, width), F32),
            jax.ShapeDtypeStruct((chips, width, cols), BF16),
            *(jax.ShapeDtypeStruct(array.shape, array.dtype) for array in consts),
        ),
        in_specs=[pl.BlockSpec(memory_space=pltpu.HBM)] * len(staged),
        out_specs=(VMEM,) * (4 + len(consts)),
        scratch_shapes=[
            *(pltpu.VMEM(array.shape, array.dtype) for array in staged[:4]),
            pltpu.VMEM((blocks * pitch, rows), F32),
            pltpu.VMEM((width, rows), F32),
            pltpu.SemaphoreType.DMA((len(staged) - 1 + chips,)),
        ],
        compiler_params=PARAMS,
        name="short",
    )(*(pltpu.with_memory_space_constraint(array, pltpu.HBM) for array in staged))
    send = send.reshape(blocks, pitch // 2, 2, rows)
    columns = lax.all_to_all(send, "ctx", split_axis=0, concat_axis=0, tiled=True, axis_index_groups=order)
    columns = columns.reshape(blocks * pitch, rows)
    conv = pl.pallas_call(
        conv_kernel,
        out_shape=jax.ShapeDtypeStruct((blocks, each, rows), BF16),
        in_specs=[VMEM] * 5,
        out_specs=VMEM,
        scratch_shapes=[
            pltpu.VMEM((blocks * pitch, rows), F32),
            pltpu.VMEM((blocks * each, rows), F32),
        ],
        compiler_params=PARAMS,
        name="conv",
    )(columns, *consts)
    conv = lax.all_to_all(conv, "ctx", split_axis=0, concat_axis=0, tiled=True, axis_index_groups=order)
    gated, given = pl.pallas_call(
        give_kernel,
        out_shape=(
            jax.ShapeDtypeStruct((rows, width), BF16),
            jax.ShapeDtypeStruct((chips, rows, cols), BF16),
        ),
        in_specs=[VMEM] * 4,
        out_specs=(VMEM, VMEM),
        compiler_params=PARAMS,
        name="give",
    )(conv, query, skip, held)
    arrived = lax.ppermute(given, "tp", [(i, i ^ 1) for i in range(shares)])
    kept = pl.pallas_call(
        keep_kernel,
        out_shape=jax.ShapeDtypeStruct((chips, rows, cols), F32),
        in_specs=[VMEM, pl.BlockSpec(memory_space=pltpu.HBM)],
        out_specs=VMEM,
        scratch_shapes=[pltpu.VMEM((chips, width, cols), BF16), pltpu.SemaphoreType.DMA((chips,))],
        compiler_params=PARAMS,
        name="keep",
    )(gated, pltpu.with_memory_space_constraint(out_weight, pltpu.HBM))
    partial = pl.pallas_call(
        pair_kernel,
        out_shape=jax.ShapeDtypeStruct((chips, rows, cols), BF16),
        in_specs=[VMEM] * 2,
        out_specs=VMEM,
        compiler_params=PARAMS,
        name="pair",
    )(kept, arrived)
    columns_of = [[2 * y + core for y in range(chips)] for core in range(2)]
    partial = lax.all_to_all(
        partial, "tp", split_axis=0, concat_axis=0, tiled=True, axis_index_groups=columns_of
    )
    return pl.pallas_call(
        sum_kernel,
        out_shape=jax.ShapeDtypeStruct((rows, cols), BF16),
        in_specs=[VMEM],
        out_specs=VMEM,
        compiler_params=PARAMS,
        name="total",
    )(partial)


def solution(mesh):
    in_specs = (P("ctx", None, "tp"), P(None, None, "tp"), P("ctx", "tp"), P("tp"), P("tp", None))
    out_specs = P("ctx", "tp")
    return jax.shard_map(body, mesh=mesh, in_specs=in_specs, out_specs=out_specs, check_vma=False)
```

```python
import functools
import math

import jax
import jax.numpy as jnp
import numpy as np
from jax import lax
from jax.experimental import pallas as pl
from jax.experimental.pallas import tpu as pltpu
from jax.sharding import PartitionSpec as P

F32 = jnp.float32
BF16 = jnp.bfloat16
VMEM = pl.BlockSpec(memory_space=pltpu.VMEM)
RIM = 16
SIDE = 4
PARAMS = pltpu.CompilerParams(vmem_limit_bytes=24 * 1024 * 1024)


def halves(table):
    high = table.astype(BF16)
    low = (table - high.astype(np.float32)).astype(BF16)
    return high, low


def block_order(blocks):
    deep = blocks // SIDE
    z = (np.arange(deep)[::-1] + 5 * deep // 8) % deep
    return (SIDE * z[None, :] + np.arange(SIDE)[::-1][:, None]).reshape(-1)


def tables(blocks, rows):
    length = blocks * rows
    freq = np.arange(blocks) + 0.25
    outer = 2.0 * math.pi * freq[:, None] * block_order(blocks)[None, :] / blocks
    first = np.concatenate([np.cos(outer), -np.sin(outer)], axis=0).astype(np.float32)
    last = (np.concatenate([np.cos(outer.T), -np.sin(outer.T)], axis=1) / length).astype(np.float32)
    turn = 2.0 * math.pi * freq[:, None] * np.arange(rows)[None, :] / length
    twist = np.stack([np.cos(turn), np.sin(turn)]).astype(np.float32)
    inner = 2.0 * math.pi * (np.outer(np.arange(rows), np.arange(rows)) % rows) / rows
    cos, sin = np.cos(inner), np.sin(inner)
    forward = np.block([[cos, -sin], [sin, cos]]).astype(np.float32)
    order = block_order(blocks)
    previous = (order[:, None] == order[None, :] + 1).astype(BF16)
    first_hi, first_lo = halves(first)
    last_hi, last_lo = halves(last)
    forward_hi, forward_lo = halves(forward)
    return (
        previous,
        np.concatenate([first_hi, first_lo], axis=1),
        twist,
        np.stack([forward_hi, forward_lo]),
        np.concatenate([last_hi, last_hi, last_lo], axis=1),
    )


def transform(value, matrix):
    high, low = split(value)
    total = jnp.dot(high, matrix[0], preferred_element_type=F32)
    total += jnp.dot(low, matrix[0], preferred_element_type=F32)
    return total + jnp.dot(high, matrix[1], preferred_element_type=F32)


def split(value):
    high = value.astype(BF16)
    return high, (value - high.astype(F32)).astype(BF16)


def load_all(sources, targets, sems):
    copies = [
        pltpu.make_async_copy(source, target, sems.at[i])
        for i, (source, target) in enumerate(zip(sources, targets))
    ]
    for copy in copies:
        copy.start()
    return copies


def columns_of_core(weight, chips, partner):
    cols = weight.shape[1] // (2 * chips)
    core = lax.rem(lax.axis_index("tp") + partner, 2)
    return [weight.at[:, pl.ds(pl.multiple_of((2 * y + core) * cols, cols), cols)] for y in reversed(range(chips))]


def short_kernel(count, *refs):
    inputs, weight = refs[: count - 1], refs[count - 1]
    (send, query, skip, held), tables = refs[count : count + 4], refs[count + 4 : 2 * count - 1]
    features, taps, filt, bias, wide, corner, sems = refs[2 * count - 1 :]
    chips = held.shape[0]
    sources = [*inputs, *columns_of_core(weight, chips, 1)]
    copies = load_all(sources, (features, taps, filt, bias, *tables, *(held.at[y] for y in range(chips))), sems)
    for copy in copies[:4]:
        copy.wait()
    rows, width = filt.shape
    each = RIM // 2
    groups = width // each
    pitch = send.shape[0] // groups
    row = lax.broadcasted_iota(jnp.int32, (rows, width), 0)

    def stream(j):
        current = features[j].astype(F32)
        one = jnp.where(row == 0, 0.0, pltpu.roll(current, 1, 0))
        two = jnp.where(row < 2, 0.0, pltpu.roll(current, 2, 0))
        near, far = taps[1, j : j + 1], taps[2, j : j + 1]
        after = [near * current[rows - 1 :] + far * current[rows - 2 : rows - 1], far * current[rows - 1 :]]
        return taps[0, j : j + 1] * current + near * one + far * two, after

    asked, asked_after = stream(0)
    key, key_after = stream(1)
    value, value_after = stream(2)
    gate = key * value
    edge = [key[:2], value[:2], asked[:2], *key_after, *value_after, *asked_after, bias[...], bias[...]]
    edge = jnp.concatenate([*edge, jnp.zeros((RIM - 14, width), F32)], axis=0)
    corner[:, :RIM] = edge.T
    lane = lax.broadcasted_iota(jnp.int32, (groups, rows), 1)
    packed = jnp.zeros((groups, rows), F32)
    for ch in range(each):
        mine = corner[pl.ds(ch, groups, stride=each), :]
        packed += jnp.where(lane // RIM == ch, pltpu.roll(mine, RIM * ch, 1) if ch else mine, 0.0)
    gate_t, filt_t = gate.T, filt[...].T
    for group in range(groups):
        wide[pitch * group : pitch * group + each] = gate_t[each * group : each * (group + 1)]
        wide[pitch * group + each : pitch * group + 2 * each] = filt_t[each * group : each * (group + 1)]
    wide[pl.ds(2 * each, groups, stride=pitch), :] = packed
    wide[pl.ds(2 * each + 1, groups, stride=pitch), :] = jnp.zeros((groups, rows), F32)
    send[...] = wide[...].astype(send.dtype)
    query[...] = asked
    skip[...] = bias[...] * gate
    for copy in copies[4:]:
        copy.wait()


def conv_kernel(columns, previous, first, twist, forward, last, out, gathered, spread):
    each, blocks, rows = RIM // 2, out.shape[0], out.shape[2]
    both = 2 * each
    pitch = columns.shape[0] // blocks
    gathered[...] = columns[...].astype(F32)
    edge = gathered[pl.ds(both, blocks, stride=pitch), :]
    before = jnp.dot(previous[...], edge.astype(BF16), preferred_element_type=F32)
    featurized = edge + pltpu.roll(before, rows - 6, 1)
    edge_gate = featurized * pltpu.roll(featurized, rows - 2, 1)
    edge_query = pltpu.roll(featurized, rows - 4, 1)
    edge_skip = edge_query * edge_gate * pltpu.roll(edge, rows - 12, 1)
    lane = lax.broadcasted_iota(jnp.int32, edge.shape, 1)

    def channel(array, ch):
        return pltpu.roll(array, rows - RIM * ch, 1) if ch else array

    streams = [gathered[pl.ds(ch, blocks, stride=pitch), :] for ch in range(both)]
    for ch in range(each):
        streams[ch] = jnp.where(lane < 2, channel(edge_gate, ch), streams[ch])
    wide = jnp.concatenate(streams, axis=1).astype(BF16)
    outer = jnp.dot(first[...], jnp.concatenate([wide, wide], axis=0), preferred_element_type=F32)
    cos, sin = twist[0], twist[1]
    twisted = []
    for ch in range(both):
        re = outer[:blocks, ch * rows : (ch + 1) * rows]
        im = outer[blocks:, ch * rows : (ch + 1) * rows]
        twisted.append(jnp.concatenate([re * cos + im * sin, im * cos - re * sin], axis=1))
    spectrum = transform(jnp.concatenate(twisted, axis=0), forward)
    gate, filt = spectrum[: each * blocks], spectrum[each * blocks :]
    gate_re, gate_im = gate[:, :rows], gate[:, rows:]
    filt_re, filt_im = filt[:, :rows], filt[:, rows:]
    product = [gate_re * filt_re - gate_im * filt_im, -gate_re * filt_im - gate_im * filt_re]
    inner = transform(jnp.concatenate(product, axis=1), forward)
    turned = []
    for ch in range(each):
        re = inner[ch * blocks : (ch + 1) * blocks, :rows]
        im = inner[ch * blocks : (ch + 1) * blocks, rows:]
        turned.append(jnp.concatenate([re * cos + im * sin, re * sin - im * cos], axis=0))
    high, low = split(jnp.concatenate(turned, axis=1))
    result = jnp.dot(last[...], jnp.concatenate([high, low, high], axis=0), preferred_element_type=F32)
    for ch in range(each):
        part = result[:, ch * rows : (ch + 1) * rows]
        finished = channel(edge_query, ch) * part + channel(edge_skip, ch)
        spread[pl.ds(ch, blocks, stride=each), :] = jnp.where(lane < 2, finished, part)
    out[...] = spread[...].reshape(out.shape).astype(out.dtype)


def give_kernel(conv, query, skip, weight, gated, given):
    arrived = conv[...].astype(F32).reshape(query.shape[::-1]).T
    row = lax.broadcasted_iota(jnp.int32, query.shape, 0)
    finished = jnp.where(row < 2, arrived, query[...] * (arrived + skip[...]))
    gated[...] = finished.astype(gated.dtype)
    for y in range(given.shape[0]):
        given[y] = jnp.dot(gated[...], weight[y], preferred_element_type=F32).astype(given.dtype)


def keep_kernel(gated, weight, kept, held, sems):
    chips = kept.shape[0]
    copies = load_all(columns_of_core(weight, chips, 0), [held.at[y] for y in range(chips)], sems)
    for y in range(chips):
        copies[y].wait()
        kept[y] = jnp.dot(gated[...], held[y], preferred_element_type=F32)


def pair_kernel(kept, arrived, out):
    out[...] = (kept[...] + arrived[...].astype(F32)).astype(out.dtype)


def sum_kernel(parts, out):
    out[...] = jnp.sum(parts[...].astype(F32), axis=0).astype(out.dtype)


def body(features, short_filter, long_filter, filter_bias, out_weight):
    rows, streams, width = features.shape
    blocks = lax.axis_size("ctx")
    shares = lax.axis_size("tp")
    chips = shares // 2
    each = width // blocks
    order = [[int(block) for block in block_order(blocks)]]
    cols = out_weight.shape[1] // shares
    consts = [jnp.asarray(table) for table in tables(blocks, rows)]
    planes = jnp.transpose(features, (1, 0, 2))
    staged = [planes, short_filter, long_filter, filter_bias.reshape(1, width), *consts, out_weight]
    pitch = 2 * each + 2
    send, query, skip, held, *consts = pl.pallas_call(
        functools.partial(short_kernel, len(staged)),
        out_shape=(
            jax.ShapeDtypeStruct((blocks * pitch, rows), BF16),
            jax.ShapeDtypeStruct((rows, width), F32),
            jax.ShapeDtypeStruct((rows, width), F32),
            jax.ShapeDtypeStruct((chips, width, cols), BF16),
            *(jax.ShapeDtypeStruct(array.shape, array.dtype) for array in consts),
        ),
        in_specs=[pl.BlockSpec(memory_space=pltpu.HBM)] * len(staged),
        out_specs=(VMEM,) * (4 + len(consts)),
        scratch_shapes=[
            *(pltpu.VMEM(array.shape, array.dtype) for array in staged[:4]),
            pltpu.VMEM((blocks * pitch, rows), F32),
            pltpu.VMEM((width, rows), F32),
            pltpu.SemaphoreType.DMA((len(staged) - 1 + chips,)),
        ],
        compiler_params=PARAMS,
        name="short",
    )(*(pltpu.with_memory_space_constraint(array, pltpu.HBM) for array in staged))
    send = send.reshape(blocks, pitch // 2, 2, rows)
    columns = lax.all_to_all(send, "ctx", split_axis=0, concat_axis=0, tiled=True, axis_index_groups=order)
    columns = columns.reshape(blocks * pitch, rows)
    conv = pl.pallas_call(
        conv_kernel,
        out_shape=jax.ShapeDtypeStruct((blocks, each, rows), BF16),
        in_specs=[VMEM] * 6,
        out_specs=VMEM,
        scratch_shapes=[
            pltpu.VMEM((blocks * pitch, rows), F32),
            pltpu.VMEM((blocks * each, rows), F32),
        ],
        compiler_params=PARAMS,
        name="conv",
    )(columns, *consts)
    conv = lax.all_to_all(conv, "ctx", split_axis=0, concat_axis=0, tiled=True, axis_index_groups=order)
    gated, given = pl.pallas_call(
        give_kernel,
        out_shape=(
            jax.ShapeDtypeStruct((rows, width), BF16),
            jax.ShapeDtypeStruct((chips, rows, cols), BF16),
        ),
        in_specs=[VMEM] * 4,
        out_specs=(VMEM, VMEM),
        compiler_params=PARAMS,
        name="give",
    )(conv, query, skip, held)
    arrived = lax.ppermute(given, "tp", [(i, i ^ 1) for i in range(shares)])
    kept = pl.pallas_call(
        keep_kernel,
        out_shape=jax.ShapeDtypeStruct((chips, rows, cols), F32),
        in_specs=[VMEM, pl.BlockSpec(memory_space=pltpu.HBM)],
        out_specs=VMEM,
        scratch_shapes=[pltpu.VMEM((chips, width, cols), BF16), pltpu.SemaphoreType.DMA((chips,))],
        compiler_params=PARAMS,
        name="keep",
    )(gated, pltpu.with_memory_space_constraint(out_weight, pltpu.HBM))
    partial = pl.pallas_call(
        pair_kernel,
        out_shape=jax.ShapeDtypeStruct((chips, rows, cols), BF16),
        in_specs=[VMEM] * 2,
        out_specs=VMEM,
        compiler_params=PARAMS,
        name="pair",
    )(kept, arrived)
    columns_of = [[2 * y + core for y in reversed(range(chips))] for core in range(2)]
    partial = lax.all_to_all(
        partial, "tp", split_axis=0, concat_axis=0, tiled=True, axis_index_groups=columns_of
    )
    return pl.pallas_call(
        sum_kernel,
        out_shape=jax.ShapeDtypeStruct((rows, cols), BF16),
        in_specs=[VMEM],
        out_specs=VMEM,
        compiler_params=PARAMS,
        name="total",
    )(partial)


def solution(mesh):
    in_specs = (P("ctx", None, "tp"), P(None, None, "tp"), P("ctx", "tp"), P("tp"), P("tp", None))
    out_specs = P("ctx", "tp")
    return jax.shard_map(body, mesh=mesh, in_specs=in_specs, out_specs=out_specs, check_vma=False)
```

```python
import functools
import math

import jax
import jax.numpy as jnp
import numpy as np
from jax import lax
from jax.experimental import pallas as pl
from jax.experimental.pallas import tpu as pltpu
from jax.sharding import PartitionSpec as P

F32 = jnp.float32
BF16 = jnp.bfloat16
VMEM = pl.BlockSpec(memory_space=pltpu.VMEM)
RIM = 16
SIDE = 4
X_ORDER = (3, 2, 1, 0)
PARAMS = pltpu.CompilerParams(vmem_limit_bytes=24 * 1024 * 1024)


def halves(table):
    high = table.astype(BF16)
    low = (table - high.astype(np.float32)).astype(BF16)
    return high, low


def z_order(deep):
    return (np.arange(deep)[::-1] + 5 * deep // 8) % deep


def block_order(blocks):
    z = z_order(blocks // SIDE)
    return (SIDE * z[None, :] + np.array(X_ORDER)[:, None]).reshape(-1)


def tables(blocks, rows):
    length = blocks * rows
    freq = np.arange(blocks) + 0.25
    outer = 2.0 * math.pi * freq[:, None] * block_order(blocks)[None, :] / blocks
    first = np.concatenate([np.cos(outer), -np.sin(outer)], axis=0).astype(np.float32)
    last = (np.concatenate([np.cos(outer.T), -np.sin(outer.T)], axis=1) / length).astype(np.float32)
    turn = 2.0 * math.pi * freq[:, None] * np.arange(rows)[None, :] / length
    twist = np.stack([np.cos(turn), np.sin(turn)]).astype(np.float32)
    inner = 2.0 * math.pi * (np.outer(np.arange(rows), np.arange(rows)) % rows) / rows
    cos, sin = np.cos(inner), np.sin(inner)
    forward = np.block([[cos, -sin], [sin, cos]]).astype(np.float32)
    first_hi, first_lo = halves(first)
    last_hi, last_lo = halves(last)
    forward_hi, forward_lo = halves(forward)
    return (
        np.concatenate([first_hi, first_lo], axis=1),
        twist,
        np.stack([forward_hi, forward_lo]),
        np.concatenate([last_hi, last_hi, last_lo], axis=1),
    )


def transform(value, matrix):
    high, low = split(value)
    total = jnp.dot(high, matrix[0], preferred_element_type=F32)
    total += jnp.dot(low, matrix[0], preferred_element_type=F32)
    return total + jnp.dot(high, matrix[1], preferred_element_type=F32)


def split(value):
    high = value.astype(BF16)
    return high, (value - high.astype(F32)).astype(BF16)


def load_all(sources, targets, sems):
    copies = [
        pltpu.make_async_copy(source, target, sems.at[i])
        for i, (source, target) in enumerate(zip(sources, targets))
    ]
    for copy in copies:
        copy.start()
    return copies


def columns_of_core(weight, chips, partner):
    cols = weight.shape[1] // (2 * chips)
    core = lax.rem(lax.axis_index("tp") + partner, 2)
    return [weight.at[:, pl.ds(pl.multiple_of((2 * y + core) * cols, cols), cols)] for y in reversed(range(chips))]


def short_kernel(count, *refs):
    inputs, weight = refs[: count - 1], refs[count - 1]
    (send, query, skip, held), tables = refs[count : count + 4], refs[count + 4 : 2 * count - 1]
    features, taps, filt, bias, wide, corner, sems = refs[2 * count - 1 :]
    chips = held.shape[0]
    sources = [*inputs, *columns_of_core(weight, chips, 1)]
    copies = load_all(sources, (features, taps, filt, bias, *tables, *(held.at[y] for y in range(chips))), sems)
    for copy in copies[:4]:
        copy.wait()
    rows, width = filt.shape
    each = RIM // 2
    groups = width // each
    pitch = send.shape[0] // groups
    row = lax.broadcasted_iota(jnp.int32, (rows, width), 0)

    def stream(j):
        current = features[j].astype(F32)
        one = jnp.where(row == 0, 0.0, pltpu.roll(current, 1, 0))
        two = jnp.where(row < 2, 0.0, pltpu.roll(current, 2, 0))
        near, far = taps[1, j : j + 1], taps[2, j : j + 1]
        after = [near * current[rows - 1 :] + far * current[rows - 2 : rows - 1], far * current[rows - 1 :]]
        return taps[0, j : j + 1] * current + near * one + far * two, after

    asked, asked_after = stream(0)
    key, key_after = stream(1)
    value, value_after = stream(2)
    gate = key * value
    edge = [key[:2], value[:2], asked[:2], *key_after, *value_after, *asked_after, bias[...], bias[...]]
    edge = jnp.concatenate([*edge, jnp.zeros((RIM - 14, width), F32)], axis=0)
    corner[:, :RIM] = edge.T
    lane = lax.broadcasted_iota(jnp.int32, (groups, rows), 1)
    packed = jnp.zeros((groups, rows), F32)
    for ch in range(each):
        mine = corner[pl.ds(ch, groups, stride=each), :]
        packed += jnp.where(lane // RIM == ch, pltpu.roll(mine, RIM * ch, 1) if ch else mine, 0.0)
    gate_t, filt_t = gate.T, filt[...].T
    for group in range(groups):
        wide[pitch * group : pitch * group + each] = gate_t[each * group : each * (group + 1)]
        wide[pitch * group + each : pitch * group + 2 * each] = filt_t[each * group : each * (group + 1)]
    wide[pl.ds(2 * each, groups, stride=pitch), :] = packed
    wide[pl.ds(2 * each + 1, groups, stride=pitch), :] = jnp.zeros((groups, rows), F32)
    send[...] = wide[...].astype(send.dtype)
    query[...] = asked
    skip[...] = bias[...] * gate
    for copy in copies[4:]:
        copy.wait()


def conv_kernel(columns, first, twist, forward, last, out, gathered, spread):
    each, blocks, rows = RIM // 2, out.shape[0], out.shape[2]
    both = 2 * each
    pitch = columns.shape[0] // blocks
    gathered[...] = columns[...].astype(F32)
    edge = gathered[pl.ds(both, blocks, stride=pitch), :]
    deep = blocks // SIDE
    runs = {x: edge[deep * i : deep * (i + 1)] for i, x in enumerate(X_ORDER)}
    start = lax.broadcasted_iota(jnp.int32, (deep, rows), 0) == z_order(deep).tolist().index(0)
    wrapped = jnp.where(start, 0.0, pltpu.roll(runs[SIDE - 1], deep - 1, 0))
    before = jnp.concatenate([runs[x - 1] if x else wrapped for x in X_ORDER], axis=0)
    featurized = edge + pltpu.roll(before, rows - 6, 1)
    edge_gate = featurized * pltpu.roll(featurized, rows - 2, 1)
    edge_query = pltpu.roll(featurized, rows - 4, 1)
    edge_skip = edge_query * edge_gate * pltpu.roll(edge, rows - 12, 1)
    lane = lax.broadcasted_iota(jnp.int32, edge.shape, 1)

    def channel(array, ch):
        return pltpu.roll(array, rows - RIM * ch, 1) if ch else array

    streams = [gathered[pl.ds(ch, blocks, stride=pitch), :] for ch in range(both)]
    for ch in range(each):
        streams[ch] = jnp.where(lane < 2, channel(edge_gate, ch), streams[ch])
    wide = jnp.concatenate(streams, axis=1).astype(BF16)
    outer = jnp.dot(first[...], jnp.concatenate([wide, wide], axis=0), preferred_element_type=F32)
    cos, sin = twist[0], twist[1]
    twisted = []
    for ch in range(both):
        re = outer[:blocks, ch * rows : (ch + 1) * rows]
        im = outer[blocks:, ch * rows : (ch + 1) * rows]
        twisted.append(jnp.concatenate([re * cos + im * sin, im * cos - re * sin], axis=1))
    spectrum = transform(jnp.concatenate(twisted, axis=0), forward)
    gate, filt = spectrum[: each * blocks], spectrum[each * blocks :]
    gate_re, gate_im = gate[:, :rows], gate[:, rows:]
    filt_re, filt_im = filt[:, :rows], filt[:, rows:]
    product = [gate_re * filt_re - gate_im * filt_im, -gate_re * filt_im - gate_im * filt_re]
    inner = transform(jnp.concatenate(product, axis=1), forward)
    turned = []
    for ch in range(each):
        re = inner[ch * blocks : (ch + 1) * blocks, :rows]
        im = inner[ch * blocks : (ch + 1) * blocks, rows:]
        turned.append(jnp.concatenate([re * cos + im * sin, re * sin - im * cos], axis=0))
    high, low = split(jnp.concatenate(turned, axis=1))
    result = jnp.dot(last[...], jnp.concatenate([high, low, high], axis=0), preferred_element_type=F32)
    for ch in range(each):
        part = result[:, ch * rows : (ch + 1) * rows]
        finished = channel(edge_query, ch) * part + channel(edge_skip, ch)
        spread[pl.ds(ch, blocks, stride=each), :] = jnp.where(lane < 2, finished, part)
    out[...] = spread[...].reshape(out.shape).astype(out.dtype)


def give_kernel(conv, query, skip, weight, gated, given):
    arrived = conv[...].astype(F32).reshape(query.shape[::-1]).T
    row = lax.broadcasted_iota(jnp.int32, query.shape, 0)
    finished = jnp.where(row < 2, arrived, query[...] * (arrived + skip[...]))
    gated[...] = finished.astype(gated.dtype)
    for y in range(given.shape[0]):
        given[y] = jnp.dot(gated[...], weight[y], preferred_element_type=F32).astype(given.dtype)


def keep_kernel(gated, weight, kept, held, sems):
    chips = kept.shape[0]
    copies = load_all(columns_of_core(weight, chips, 0), [held.at[y] for y in range(chips)], sems)
    for y in range(chips):
        copies[y].wait()
        kept[y] = jnp.dot(gated[...], held[y], preferred_element_type=F32)


def pair_kernel(kept, arrived, out):
    out[...] = (kept[...] + arrived[...].astype(F32)).astype(out.dtype)


def sum_kernel(parts, out):
    out[...] = jnp.sum(parts[...].astype(F32), axis=0).astype(out.dtype)


def body(features, short_filter, long_filter, filter_bias, out_weight):
    rows, streams, width = features.shape
    blocks = lax.axis_size("ctx")
    shares = lax.axis_size("tp")
    chips = shares // 2
    each = width // blocks
    order = [[int(block) for block in block_order(blocks)]]
    cols = out_weight.shape[1] // shares
    consts = [jnp.asarray(table) for table in tables(blocks, rows)]
    planes = jnp.transpose(features, (1, 0, 2))
    staged = [planes, short_filter, long_filter, filter_bias.reshape(1, width), *consts, out_weight]
    pitch = 2 * each + 2
    send, query, skip, held, *consts = pl.pallas_call(
        functools.partial(short_kernel, len(staged)),
        out_shape=(
            jax.ShapeDtypeStruct((blocks * pitch, rows), BF16),
            jax.ShapeDtypeStruct((rows, width), F32),
            jax.ShapeDtypeStruct((rows, width), F32),
            jax.ShapeDtypeStruct((chips, width, cols), BF16),
            *(jax.ShapeDtypeStruct(array.shape, array.dtype) for array in consts),
        ),
        in_specs=[pl.BlockSpec(memory_space=pltpu.HBM)] * len(staged),
        out_specs=(VMEM,) * (4 + len(consts)),
        scratch_shapes=[
            *(pltpu.VMEM(array.shape, array.dtype) for array in staged[:4]),
            pltpu.VMEM((blocks * pitch, rows), F32),
            pltpu.VMEM((width, rows), F32),
            pltpu.SemaphoreType.DMA((len(staged) - 1 + chips,)),
        ],
        compiler_params=PARAMS,
        name="short",
    )(*(pltpu.with_memory_space_constraint(array, pltpu.HBM) for array in staged))
    send = send.reshape(blocks, pitch // 2, 2, rows)
    columns = lax.all_to_all(send, "ctx", split_axis=0, concat_axis=0, tiled=True, axis_index_groups=order)
    columns = columns.reshape(blocks * pitch, rows)
    conv = pl.pallas_call(
        conv_kernel,
        out_shape=jax.ShapeDtypeStruct((blocks, each, rows), BF16),
        in_specs=[VMEM] * 5,
        out_specs=VMEM,
        scratch_shapes=[
            pltpu.VMEM((blocks * pitch, rows), F32),
            pltpu.VMEM((blocks * each, rows), F32),
        ],
        compiler_params=PARAMS,
        name="conv",
    )(columns, *consts)
    conv = lax.all_to_all(conv, "ctx", split_axis=0, concat_axis=0, tiled=True, axis_index_groups=order)
    gated, given = pl.pallas_call(
        give_kernel,
        out_shape=(
            jax.ShapeDtypeStruct((rows, width), BF16),
            jax.ShapeDtypeStruct((chips, rows, cols), BF16),
        ),
        in_specs=[VMEM] * 4,
        out_specs=(VMEM, VMEM),
        compiler_params=PARAMS,
        name="give",
    )(conv, query, skip, held)
    arrived = lax.ppermute(given, "tp", [(i, i ^ 1) for i in range(shares)])
    kept = pl.pallas_call(
        keep_kernel,
        out_shape=jax.ShapeDtypeStruct((chips, rows, cols), F32),
        in_specs=[VMEM, pl.BlockSpec(memory_space=pltpu.HBM)],
        out_specs=VMEM,
        scratch_shapes=[pltpu.VMEM((chips, width, cols), BF16), pltpu.SemaphoreType.DMA((chips,))],
        compiler_params=PARAMS,
        name="keep",
    )(gated, pltpu.with_memory_space_constraint(out_weight, pltpu.HBM))
    partial = pl.pallas_call(
        pair_kernel,
        out_shape=jax.ShapeDtypeStruct((chips, rows, cols), BF16),
        in_specs=[VMEM] * 2,
        out_specs=VMEM,
        compiler_params=PARAMS,
        name="pair",
    )(kept, arrived)
    columns_of = [[2 * y + core for y in reversed(range(chips))] for core in range(2)]
    partial = lax.all_to_all(
        partial, "tp", split_axis=0, concat_axis=0, tiled=True, axis_index_groups=columns_of
    )
    return pl.pallas_call(
        sum_kernel,
        out_shape=jax.ShapeDtypeStruct((rows, cols), BF16),
        in_specs=[VMEM],
        out_specs=VMEM,
        compiler_params=PARAMS,
        name="total",
    )(partial)


def solution(mesh):
    in_specs = (P("ctx", None, "tp"), P(None, None, "tp"), P("ctx", "tp"), P("tp"), P("tp", None))
    out_specs = P("ctx", "tp")
    return jax.shard_map(body, mesh=mesh, in_specs=in_specs, out_specs=out_specs, check_vma=False)
```

```python
import functools
import math

import jax
import jax.numpy as jnp
import numpy as np
from jax import lax
from jax.experimental import pallas as pl
from jax.experimental.pallas import tpu as pltpu
from jax.sharding import PartitionSpec as P

F32 = jnp.float32
BF16 = jnp.bfloat16
VMEM = pl.BlockSpec(memory_space=pltpu.VMEM)
RIM = 16
SIDE = 4
X_ORDER = (2, 1, 0, 3)
PARAMS = pltpu.CompilerParams(vmem_limit_bytes=24 * 1024 * 1024)


def halves(table):
    high = table.astype(BF16)
    low = (table - high.astype(np.float32)).astype(BF16)
    return high, low


def z_order(deep):
    return (np.arange(deep)[::-1] + 5 * deep // 8) % deep


def block_order(blocks):
    z = z_order(blocks // SIDE)
    return (SIDE * z[None, :] + np.array(X_ORDER)[:, None]).reshape(-1)


def tables(blocks, rows):
    length = blocks * rows
    freq = np.arange(blocks) + 0.25
    outer = 2.0 * math.pi * freq[:, None] * block_order(blocks)[None, :] / blocks
    first = np.concatenate([np.cos(outer), -np.sin(outer)], axis=0).astype(np.float32)
    last = (np.concatenate([np.cos(outer.T), -np.sin(outer.T)], axis=1) / length).astype(np.float32)
    turn = 2.0 * math.pi * freq[:, None] * np.arange(rows)[None, :] / length
    twist = np.stack([np.cos(turn), np.sin(turn)]).astype(np.float32)
    inner = 2.0 * math.pi * (np.outer(np.arange(rows), np.arange(rows)) % rows) / rows
    cos, sin = np.cos(inner), np.sin(inner)
    forward = np.block([[cos, -sin], [sin, cos]]).astype(np.float32)
    first_hi, first_lo = halves(first)
    last_hi, last_lo = halves(last)
    forward_hi, forward_lo = halves(forward)
    return (
        np.concatenate([first_hi, first_lo], axis=1),
        twist,
        np.stack([forward_hi, forward_lo]),
        np.concatenate([last_hi, last_hi, last_lo], axis=1),
    )


def transform(value, matrix):
    high, low = split(value)
    total = jnp.dot(high, matrix[0], preferred_element_type=F32)
    total += jnp.dot(low, matrix[0], preferred_element_type=F32)
    return total + jnp.dot(high, matrix[1], preferred_element_type=F32)


def split(value):
    high = value.astype(BF16)
    return high, (value - high.astype(F32)).astype(BF16)


def load_all(sources, targets, sems):
    copies = [
        pltpu.make_async_copy(source, target, sems.at[i])
        for i, (source, target) in enumerate(zip(sources, targets))
    ]
    for copy in copies:
        copy.start()
    return copies


def columns_of_core(weight, chips, partner):
    cols = weight.shape[1] // (2 * chips)
    core = lax.rem(lax.axis_index("tp") + partner, 2)
    return [weight.at[:, pl.ds(pl.multiple_of((2 * y + core) * cols, cols), cols)] for y in reversed(range(chips))]


def short_kernel(count, *refs):
    inputs, weight = refs[: count - 1], refs[count - 1]
    (send, query, skip, held), tables = refs[count : count + 4], refs[count + 4 : 2 * count - 1]
    features, taps, filt, bias, wide, corner, sems = refs[2 * count - 1 :]
    chips = held.shape[0]
    sources = [*inputs, *columns_of_core(weight, chips, 1)]
    copies = load_all(sources, (features, taps, filt, bias, *tables, *(held.at[y] for y in range(chips))), sems)
    for copy in copies[:4]:
        copy.wait()
    rows, width = filt.shape
    each = RIM // 2
    groups = width // each
    pitch = send.shape[0] // groups
    row = lax.broadcasted_iota(jnp.int32, (rows, width), 0)

    def stream(j):
        current = features[j].astype(F32)
        one = jnp.where(row == 0, 0.0, pltpu.roll(current, 1, 0))
        two = jnp.where(row < 2, 0.0, pltpu.roll(current, 2, 0))
        near, far = taps[1, j : j + 1], taps[2, j : j + 1]
        after = [near * current[rows - 1 :] + far * current[rows - 2 : rows - 1], far * current[rows - 1 :]]
        return taps[0, j : j + 1] * current + near * one + far * two, after

    asked, asked_after = stream(0)
    key, key_after = stream(1)
    value, value_after = stream(2)
    gate = key * value
    edge = [key[:2], value[:2], asked[:2], *key_after, *value_after, *asked_after, bias[...], bias[...]]
    edge = jnp.concatenate([*edge, jnp.zeros((RIM - 14, width), F32)], axis=0)
    corner[:, :RIM] = edge.T
    lane = lax.broadcasted_iota(jnp.int32, (groups, rows), 1)
    packed = jnp.zeros((groups, rows), F32)
    for ch in range(each):
        mine = corner[pl.ds(ch, groups, stride=each), :]
        packed += jnp.where(lane // RIM == ch, pltpu.roll(mine, RIM * ch, 1) if ch else mine, 0.0)
    gate_t, filt_t = gate.T, filt[...].T
    for group in range(groups):
        wide[pitch * group : pitch * group + each] = gate_t[each * group : each * (group + 1)]
        wide[pitch * group + each : pitch * group + 2 * each] = filt_t[each * group : each * (group + 1)]
    wide[pl.ds(2 * each, groups, stride=pitch), :] = packed
    wide[pl.ds(2 * each + 1, groups, stride=pitch), :] = jnp.zeros((groups, rows), F32)
    send[...] = wide[...].astype(send.dtype)
    query[...] = asked
    skip[...] = bias[...] * gate
    for copy in copies[4:]:
        copy.wait()


def conv_kernel(columns, first, twist, forward, last, out, gathered, spread):
    each, blocks, rows = RIM // 2, out.shape[0], out.shape[2]
    both = 2 * each
    pitch = columns.shape[0] // blocks
    gathered[...] = columns[...].astype(F32)
    edge = gathered[pl.ds(both, blocks, stride=pitch), :]
    deep = blocks // SIDE
    runs = {x: edge[deep * i : deep * (i + 1)] for i, x in enumerate(X_ORDER)}
    start = lax.broadcasted_iota(jnp.int32, (deep, rows), 0) == z_order(deep).tolist().index(0)
    wrapped = jnp.where(start, 0.0, pltpu.roll(runs[SIDE - 1], deep - 1, 0))
    before = jnp.concatenate([runs[x - 1] if x else wrapped for x in X_ORDER], axis=0)
    featurized = edge + pltpu.roll(before, rows - 6, 1)
    edge_gate = featurized * pltpu.roll(featurized, rows - 2, 1)
    edge_query = pltpu.roll(featurized, rows - 4, 1)
    edge_skip = edge_query * edge_gate * pltpu.roll(edge, rows - 12, 1)
    lane = lax.broadcasted_iota(jnp.int32, edge.shape, 1)

    def channel(array, ch):
        return pltpu.roll(array, rows - RIM * ch, 1) if ch else array

    streams = [gathered[pl.ds(ch, blocks, stride=pitch), :] for ch in range(both)]
    for ch in range(each):
        streams[ch] = jnp.where(lane < 2, channel(edge_gate, ch), streams[ch])
    wide = jnp.concatenate(streams, axis=1).astype(BF16)
    outer = jnp.dot(first[...], jnp.concatenate([wide, wide], axis=0), preferred_element_type=F32)
    cos, sin = twist[0], twist[1]
    twisted = []
    for ch in range(both):
        re = outer[:blocks, ch * rows : (ch + 1) * rows]
        im = outer[blocks:, ch * rows : (ch + 1) * rows]
        twisted.append(jnp.concatenate([re * cos + im * sin, im * cos - re * sin], axis=1))
    spectrum = transform(jnp.concatenate(twisted, axis=0), forward)
    gate, filt = spectrum[: each * blocks], spectrum[each * blocks :]
    gate_re, gate_im = gate[:, :rows], gate[:, rows:]
    filt_re, filt_im = filt[:, :rows], filt[:, rows:]
    product = [gate_re * filt_re - gate_im * filt_im, -gate_re * filt_im - gate_im * filt_re]
    inner = transform(jnp.concatenate(product, axis=1), forward)
    turned = []
    for ch in range(each):
        re = inner[ch * blocks : (ch + 1) * blocks, :rows]
        im = inner[ch * blocks : (ch + 1) * blocks, rows:]
        turned.append(jnp.concatenate([re * cos + im * sin, re * sin - im * cos], axis=0))
    high, low = split(jnp.concatenate(turned, axis=1))
    result = jnp.dot(last[...], jnp.concatenate([high, low, high], axis=0), preferred_element_type=F32)
    for ch in range(each):
        part = result[:, ch * rows : (ch + 1) * rows]
        finished = channel(edge_query, ch) * part + channel(edge_skip, ch)
        spread[pl.ds(ch, blocks, stride=each), :] = jnp.where(lane < 2, finished, part)
    out[...] = spread[...].reshape(out.shape).astype(out.dtype)


def give_kernel(conv, query, skip, weight, gated, given):
    arrived = conv[...].astype(F32).reshape(query.shape[::-1]).T
    row = lax.broadcasted_iota(jnp.int32, query.shape, 0)
    finished = jnp.where(row < 2, arrived, query[...] * (arrived + skip[...]))
    gated[...] = finished.astype(gated.dtype)
    for y in range(given.shape[0]):
        given[y] = jnp.dot(gated[...], weight[y], preferred_element_type=F32).astype(given.dtype)


def keep_kernel(gated, weight, kept, held, sems):
    chips = kept.shape[0]
    copies = load_all(columns_of_core(weight, chips, 0), [held.at[y] for y in range(chips)], sems)
    for y in range(chips):
        copies[y].wait()
        kept[y] = jnp.dot(gated[...], held[y], preferred_element_type=F32)


def pair_kernel(kept, arrived, out):
    out[...] = (kept[...] + arrived[...].astype(F32)).astype(out.dtype)


def sum_kernel(parts, out):
    out[...] = jnp.sum(parts[...].astype(F32), axis=0).astype(out.dtype)


def body(features, short_filter, long_filter, filter_bias, out_weight):
    rows, streams, width = features.shape
    blocks = lax.axis_size("ctx")
    shares = lax.axis_size("tp")
    chips = shares // 2
    each = width // blocks
    order = [[int(block) for block in block_order(blocks)]]
    cols = out_weight.shape[1] // shares
    consts = [jnp.asarray(table) for table in tables(blocks, rows)]
    planes = jnp.transpose(features, (1, 0, 2))
    staged = [planes, short_filter, long_filter, filter_bias.reshape(1, width), *consts, out_weight]
    pitch = 2 * each + 2
    send, query, skip, held, *consts = pl.pallas_call(
        functools.partial(short_kernel, len(staged)),
        out_shape=(
            jax.ShapeDtypeStruct((blocks * pitch, rows), BF16),
            jax.ShapeDtypeStruct((rows, width), F32),
            jax.ShapeDtypeStruct((rows, width), F32),
            jax.ShapeDtypeStruct((chips, width, cols), BF16),
            *(jax.ShapeDtypeStruct(array.shape, array.dtype) for array in consts),
        ),
        in_specs=[pl.BlockSpec(memory_space=pltpu.HBM)] * len(staged),
        out_specs=(VMEM,) * (4 + len(consts)),
        scratch_shapes=[
            *(pltpu.VMEM(array.shape, array.dtype) for array in staged[:4]),
            pltpu.VMEM((blocks * pitch, rows), F32),
            pltpu.VMEM((width, rows), F32),
            pltpu.SemaphoreType.DMA((len(staged) - 1 + chips,)),
        ],
        compiler_params=PARAMS,
        name="short",
    )(*(pltpu.with_memory_space_constraint(array, pltpu.HBM) for array in staged))
    send = send.reshape(blocks, pitch // 2, 2, rows)
    columns = lax.all_to_all(send, "ctx", split_axis=0, concat_axis=0, tiled=True, axis_index_groups=order)
    columns = columns.reshape(blocks * pitch, rows)
    conv = pl.pallas_call(
        conv_kernel,
        out_shape=jax.ShapeDtypeStruct((blocks, each, rows), BF16),
        in_specs=[VMEM] * 5,
        out_specs=VMEM,
        scratch_shapes=[
            pltpu.VMEM((blocks * pitch, rows), F32),
            pltpu.VMEM((blocks * each, rows), F32),
        ],
        compiler_params=PARAMS,
        name="conv",
    )(columns, *consts)
    conv = lax.all_to_all(conv, "ctx", split_axis=0, concat_axis=0, tiled=True, axis_index_groups=order)
    gated, given = pl.pallas_call(
        give_kernel,
        out_shape=(
            jax.ShapeDtypeStruct((rows, width), BF16),
            jax.ShapeDtypeStruct((chips, rows, cols), BF16),
        ),
        in_specs=[VMEM] * 4,
        out_specs=(VMEM, VMEM),
        compiler_params=PARAMS,
        name="give",
    )(conv, query, skip, held)
    arrived = lax.ppermute(given, "tp", [(i, i ^ 1) for i in range(shares)])
    kept = pl.pallas_call(
        keep_kernel,
        out_shape=jax.ShapeDtypeStruct((chips, rows, cols), F32),
        in_specs=[VMEM, pl.BlockSpec(memory_space=pltpu.HBM)],
        out_specs=VMEM,
        scratch_shapes=[pltpu.VMEM((chips, width, cols), BF16), pltpu.SemaphoreType.DMA((chips,))],
        compiler_params=PARAMS,
        name="keep",
    )(gated, pltpu.with_memory_space_constraint(out_weight, pltpu.HBM))
    partial = pl.pallas_call(
        pair_kernel,
        out_shape=jax.ShapeDtypeStruct((chips, rows, cols), BF16),
        in_specs=[VMEM] * 2,
        out_specs=VMEM,
        compiler_params=PARAMS,
        name="pair",
    )(kept, arrived)
    columns_of = [[2 * y + core for y in reversed(range(chips))] for core in range(2)]
    partial = lax.all_to_all(
        partial, "tp", split_axis=0, concat_axis=0, tiled=True, axis_index_groups=columns_of
    )
    return pl.pallas_call(
        sum_kernel,
        out_shape=jax.ShapeDtypeStruct((rows, cols), BF16),
        in_specs=[VMEM],
        out_specs=VMEM,
        compiler_params=PARAMS,
        name="total",
    )(partial)


def solution(mesh):
    in_specs = (P("ctx", None, "tp"), P(None, None, "tp"), P("ctx", "tp"), P("tp"), P("tp", None))
    out_specs = P("ctx", "tp")
    return jax.shard_map(body, mesh=mesh, in_specs=in_specs, out_specs=out_specs, check_vma=False)
```
